512 devices in a mesh: gz: 64 (over z, x, y_lo), gy: 8 (over y_hi, core).
Axes of the slice: x: 4, y: 8 (y_hi: 4, y_lo: 2; y = y_hi * 2 + y_lo), z: 8, core: 2. Of those that a mesh axis runs over, the one named last changes fastest.
Arguments:
- adjoint: float32 [3, 64, 1024, 1024], P(None, 'gz', None, 'gy'), may hold values from -6 to 6
- wind: bfloat16 [3, 64, 1024, 1024], P(None, 'gz', None, 'gy'), may hold values from -5 to 8
- classes: int32 [1024, 1024], P(None, 'gy'), may hold values from 0 to 15
- drag_coef: float32 [16], replicated, may hold values from 0.5 to 10
Outputs:
- adjoint_new: float32 [3, 64, 1024, 1024], P(None, 'gz', None, 'gy')
- sensitivity: float32 [16], replicated
The draws below stay inside these ranges and needn't reach their ends.
All inputs are finite; a program needn't handle non-finite values. Where the reference program divides by a largest or mean magnitude, that divisor is 1e-20 or more.
Results may differ from the reference program's by a relative error of at most 0.0035.
Values may be sent and summed in bfloat16 or wider, within the bound.
No kernel may reach another device: no remote copies, remote signals or barrier semaphores. Data moves between devices by JAX's collectives and lax.ppermute only.
A program may use at most 128 MiB of HBM per device.

```python
import math
import jax
import jax.numpy as jnp
from jax import lax

NX = 1024
NY = 1024
NCLASS = 16
NZ = 64


def draw_wind(key, part):
    noise_key = jax.random.fold_in(key, 11)
    levels = (jnp.arange(NZ, dtype=jnp.float32) + 0.5) / NZ
    profile = (0.5 + 2.5 * levels)[None, :, None, None]
    noise = jax.random.truncated_normal(noise_key, -4.5, 4.5, (3, NZ, NX, NY), jnp.float32)
    base = jnp.array([1.0, 0.0, 0.0], jnp.float32)[:, None, None, None]
    factor = jnp.array([0.35, 0.35, 0.3], jnp.float32)[:, None, None, None]
    return (profile * (base + factor * noise)).astype(jnp.bfloat16)


def plant(drawn, stream_key, low, largest):
    longest = drawn.shape.index(max(drawn.shape))
    spots = []
    for shift in (0, 1):
        where = [jax.random.randint(jax.random.fold_in(stream_key, axis), (), 0, length) for axis, length in enumerate(drawn.shape)]
        where[longest] = (where[longest] + shift) % drawn.shape[longest]
        spots.append(tuple(where))
    return drawn.at[spots[0]].set(low).at[spots[1]].set(largest)


def level_of(own_key, shape, shards, low, top_value):
    level, own = 1.0, jax.random.fold_in(own_key, 6)
    for axis_at, parts in shards:
        steps = jnp.exp(jax.random.uniform(jax.random.fold_in(own, axis_at), (parts,), jnp.float32, low / len(shards), top_value / len(shards)))
        level = level * jnp.repeat(steps, shape[axis_at] // parts).reshape([-1 if axis == axis_at else 1 for axis in range(len(shape))])
    return level


def bell_draw(rng, shape, width, limit, cuts=(), held_as=jnp.bfloat16):
    loudness = level_of(rng, shape, cuts, -0.22, 0.18) if cuts else 1.0
    drawn = jax.random.normal(rng, shape, jnp.float32) * width * loudness
    return jnp.minimum(jnp.maximum(drawn, -limit), limit).astype(held_as)


def setup_inputs(seed: int = 0) -> dict:
    splits = jax.random.split(jax.random.key(seed), 5)
    return {
        "adjoint": bell_draw(splits[0], (3, NZ, NX, NY), 1.0, 6.0, ((1, 64), (3, 8)), jnp.float32),
        "wind": draw_wind(jax.random.fold_in(splits[4], 71), 0),
        "classes": plant(jax.random.randint(splits[2], (NX, NY), 0, NCLASS), jax.random.fold_in(splits[2], 1), 0, NCLASS - 1).astype(jnp.int32),
        "drag_coef": jnp.clip(jnp.exp(jax.random.uniform(splits[3], (NCLASS,), jnp.float32, math.log(0.5), math.log(10.0))), 0.5, 10.0),
    }


viscosity = 0.3
courant = 0.8
epsilon = 1e-06

def spectral_tables(length):
    half_len = length // 2
    modes = jnp.arange(half_len, dtype=jnp.int32)
    points = jnp.arange(length, dtype=jnp.int32)
    phase_idx = modes[:, None] * points[None, :] % length
    angles = 2.0 * math.pi / length * phase_idx.astype(jnp.float32)
    cosine = jnp.cos(angles)
    sine = jnp.sin(angles)
    forward = jnp.concatenate([cosine, -sine], axis=0).astype(jnp.bfloat16)
    wave = 2.0 * math.pi / length * modes.astype(jnp.float32)
    weight = jnp.where(modes == 0, jnp.float32(1.0), jnp.float32(2.0)) / length
    first = jnp.concatenate([-(weight * wave)[:, None] * sine, -(weight * wave)[:, None] * cosine], axis=0)
    second = jnp.concatenate([-(weight * wave * wave)[:, None] * cosine, (weight * wave * wave)[:, None] * sine], axis=0)
    inverse = jnp.concatenate([first.T, second.T], axis=0).astype(jnp.bfloat16)
    return (forward, inverse)

def reference(adjoint, wind, classes, drag_coef):
    fwd_x, inv_x = spectral_tables(NX)
    fwd_y, inv_y = spectral_tables(NY)
    fwd_x32 = fwd_x.astype(jnp.float32)
    inv_x32 = inv_x.astype(jnp.float32)
    fwd_y32 = fwd_y.astype(jnp.float32)
    inv_y32 = inv_y.astype(jnp.float32)
    top = jnp.max(lax.optimization_barrier(jnp.sum(jnp.abs(wind.astype(jnp.float32)), axis=0)))
    step = courant / (top + epsilon)
    onehot = classes[None] == jnp.arange(NCLASS, dtype=jnp.int32)[:, None, None]
    drag = lax.optimization_barrier(jnp.sum(jnp.where(onehot, drag_coef[:, None, None], jnp.float32(0.0)), axis=0))
    padded = jnp.pad(adjoint, ((0, 0), (1, 1), (0, 0), (0, 0)))

    def plane(level):
        block = lax.dynamic_slice_in_dim(padded, level, 3, axis=1)
        below = block[:, 0]
        center = block[:, 1]
        above = block[:, 2]
        flow = lax.dynamic_index_in_dim(wind, level, axis=1, keepdims=False).astype(jnp.float32)
        low = center.astype(jnp.bfloat16).astype(jnp.float32)
        spec_x = jnp.einsum('jx,cxy->cjy', fwd_x32, low).astype(jnp.bfloat16).astype(jnp.float32)
        both_x = jnp.einsum('dj,cjy->cdy', inv_x32, spec_x)
        deriv_x = both_x[:, :NX]
        second_x = both_x[:, NX:]
        spec_y = jnp.einsum('cxy,jy->cxj', low, fwd_y32).astype(jnp.bfloat16).astype(jnp.float32)
        both_y = jnp.einsum('cxj,dj->cxd', spec_y, inv_y32)
        deriv_y = both_y[:, :, :NY]
        second_y = both_y[:, :, NY:]
        ydrift = (flow[1] * deriv_y + viscosity * second_y).astype(jnp.bfloat16)
        ydrift = lax.optimization_barrier(ydrift).astype(jnp.float32)
        deriv_z = (above - below) * 0.5
        second_z = above - 2.0 * center + below
        speed = jnp.sqrt(flow[0] * flow[0] + flow[1] * flow[1] + flow[2] * flow[2])
        height = jnp.exp(-2.0 * (level.astype(jnp.float32) + 0.5) / NZ)
        rhs = flow[0] * deriv_x + viscosity * second_x + ydrift + flow[2] * deriv_z + viscosity * second_z - drag * height * speed * center
        fresh = center + step * rhs
        column = height * speed * lax.optimization_barrier(jnp.sum(fresh * flow, axis=0))
        partial_sum = lax.optimization_barrier(jnp.sum(jnp.where(onehot, column[None], jnp.float32(0.0)), axis=(1, 2)))
        return (fresh, partial_sum)
    levels = jnp.arange(NZ, dtype=jnp.int32)
    fresh, partials = lax.map(plane, levels)
    adjoint_new = jnp.moveaxis(fresh, 0, 1)
    scale = 1.0 / math.sqrt(NX * NY * NZ / NCLASS)
    sensitivity = -step * scale * lax.optimization_barrier(jnp.sum(partials, axis=0))
    return (adjoint_new, sensitivity)
```

```python
import functools
import math

import jax
import jax.numpy as jnp
import ml_dtypes
import numpy as np
from jax import lax
from jax.experimental import pallas as pl
from jax.experimental.pallas import tpu as pltpu
from jax.sharding import PartitionSpec as P

viscosity = 0.3
courant = 0.8
epsilon = 1e-06
LANES = 128
TILE = 256
VMEM_BYTES = 48 * 1024 * 1024
f32 = jnp.float32
bf16 = jnp.bfloat16


@functools.lru_cache(maxsize=None)
def tables(length):
    half = length // 2
    modes = np.arange(half)
    points = np.arange(length)
    angles = (2.0 * np.pi / length) * ((modes[:, None] * points[None, :]) % length)
    cosine, sine = np.cos(angles), np.sin(angles)
    forward = np.concatenate([cosine, -sine], axis=0)
    wave = (2.0 * np.pi / length) * modes
    weight = np.where(modes == 0, 1.0, 2.0) / length
    w1, w2 = (weight * wave)[:, None], (weight * wave * wave)[:, None]
    first = np.concatenate([-w1 * sine, -w1 * cosine], axis=0).T
    second = np.concatenate([-w2 * cosine, w2 * sine], axis=0).T
    low = lambda a: np.ascontiguousarray(a).astype(ml_dtypes.bfloat16)
    return low(forward), low(first), low(second)


def params(sem="arbitrary", n=1):
    return pltpu.CompilerParams(dimension_semantics=(sem,) * n, vmem_limit_bytes=VMEM_BYTES)


def full(shape):
    return pl.BlockSpec(shape, lambda i: (0,) * len(shape))


SMEM = pl.BlockSpec(memory_space=pltpu.SMEM)


def dot(a, b):
    return jnp.dot(a, b, preferred_element_type=f32)


def pack_kernel(adj, wind, send, *lows):
    for c in range(3):
        low = adj[c].astype(bf16)
        send[0, c] = low
        lows[c][...] = low
    send[0, 3] = wind[0]


def pack(adj, wind, parts):
    _, nx, ny = adj.shape
    rows = nx // parts
    return pl.pallas_call(
        pack_kernel,
        grid=(parts,),
        in_specs=[
            pl.BlockSpec((3, rows, ny), lambda i: (0, i, 0)),
            pl.BlockSpec((1, rows, ny), lambda i: (1, i, 0)),
        ],
        out_specs=[pl.BlockSpec((1, 4, rows, ny), lambda i: (i, 0, 0, 0))]
        + [pl.BlockSpec((rows, ny), lambda i: (i, 0))] * 3,
        out_shape=[jax.ShapeDtypeStruct((parts, 4, rows, ny), bf16)]
        + [jax.ShapeDtypeStruct((nx, ny), bf16)] * 3,
        compiler_params=params(),
        cost_estimate=pl.CostEstimate(flops=0, bytes_accessed=nx * ny * 24, transcendentals=0),
        name="pack",
    )(adj, wind)


def class_sums(column, cls, acc, count):
    for k in range(count):
        kept = jnp.where(cls == k, column, 0.0)
        acc[k] += jnp.sum(kept.reshape(-1, 8, kept.shape[-1]), axis=0)


def to_lanes(acc, count, offset):
    per = jnp.sum(acc[...], axis=1)
    per = jnp.sum(per, axis=1, keepdims=True)
    row = lax.broadcasted_iota(jnp.int32, (count, LANES), 0)
    lane = lax.broadcasted_iota(jnp.int32, (count, LANES), 1)
    return jnp.sum(jnp.where(lane == row + offset, per, 0.0), axis=0, keepdims=True)


def x_kernel(steps, count, scal, coef, fwd, inv, l0, l1, l2, adj, wind, cls_ref, rhs, sums, low, spec, acc, top):
    i = pl.program_id(0)
    ny = l0.shape[1]

    @pl.when(i == 0)
    def _():
        for c, ref in enumerate((l0, l1, l2)):
            low[:, c * ny:(c + 1) * ny] = ref[...]
        acc[...] = jnp.zeros_like(acc)
        top[...] = jnp.zeros_like(top)

    @pl.when(i < steps)
    def _():
        spec[pl.ds(pl.multiple_of(i * TILE, TILE), TILE), :] = dot(fwd[...], low[...]).astype(bf16)

    @pl.when(i >= steps)
    def _():
        dx = dot(inv[0, :TILE], spec[...])
        dxx = dot(inv[0, TILE:], spec[...])
        cls = cls_ref[...]
        w = [wind[c].astype(f32) for c in range(3)]
        speed = jnp.sqrt(w[0] * w[0] + w[1] * w[1] + w[2] * w[2])
        weight = scal[0] * speed
        drag = jnp.zeros_like(speed)
        for k in range(count):
            drag = jnp.where(cls == k, coef[k], drag)
        damp = drag * weight + 2.0 * viscosity
        total = jnp.zeros_like(speed)
        for c in range(3):
            a = adj[c]
            total += a * w[c]
            cols = slice(c * ny, (c + 1) * ny)
            rhs[c] = w[0] * dx[:, cols] + viscosity * dxx[:, cols] - damp * a
        class_sums(weight * total, cls, acc, count)
        size = jnp.abs(w[0]) + jnp.abs(w[1]) + jnp.abs(w[2])
        top[...] = jnp.maximum(top[...], jnp.max(size.reshape(-1, 8, ny), axis=0))

    @pl.when(i == pl.num_programs(0) - 1)
    def _():
        lane = lax.broadcasted_iota(jnp.int32, (1, LANES), 1)
        peak = jnp.max(jnp.max(top[...], axis=0, keepdims=True), axis=1, keepdims=True)
        sums[...] = jnp.where(lane == 2 * count, peak, to_lanes(acc, count, 0))


def x_part(scal, coef, fwd, inv, lows, adj, wind, classes):
    _, nx, ny = adj.shape
    count = coef.shape[0]
    steps = nx // TILE
    late = lambda i: jnp.maximum(i - steps, 0)
    return pl.pallas_call(
        functools.partial(x_kernel, steps, count),
        grid=(2 * steps,),
        in_specs=[SMEM, SMEM,
                  pl.BlockSpec((TILE, nx), lambda i: (jnp.minimum(i, steps - 1), 0)),
                  pl.BlockSpec((1, 2 * TILE, nx), lambda i: (late(i), 0, 0))]
        + [full((nx, ny))] * 3
        + [pl.BlockSpec((3, TILE, ny), lambda i: (0, late(i), 0)),
           pl.BlockSpec((3, TILE, ny), lambda i: (0, late(i), 0)),
           pl.BlockSpec((TILE, ny), lambda i: (late(i), 0))],
        out_specs=[pl.BlockSpec((3, TILE, ny), lambda i: (0, late(i), 0)), full((1, LANES))],
        out_shape=[jax.ShapeDtypeStruct((3, nx, ny), f32), jax.ShapeDtypeStruct((1, LANES), f32)],
        scratch_shapes=[pltpu.VMEM((nx, 3 * ny), bf16), pltpu.VMEM((nx, 3 * ny), bf16),
                        pltpu.VMEM((count, 8, ny), f32), pltpu.VMEM((8, ny), f32)],
        compiler_params=params(),
        cost_estimate=pl.CostEstimate(flops=6 * nx * nx * 3 * ny, bytes_accessed=12 * 1024 * 1024, transcendentals=0),
        name="x_part",
    )(scal, coef, fwd, inv, *lows, adj, wind, classes)


def y_kernel(steps, recv, fwd, inv, out, lines, spec):
    i = pl.program_id(0)
    parts, _, rows, ny = recv.shape

    @pl.when(i == 0)
    def _():
        for s in range(parts):
            for c in range(3):
                lines[c * rows:(c + 1) * rows, s * ny:(s + 1) * ny] = recv[s, c]

    @pl.when(i < steps)
    def _():
        spec[:, pl.ds(pl.multiple_of(i * TILE, TILE), TILE)] = dot(lines[...], fwd[...]).astype(bf16)

    @pl.when(i >= steps)
    def _():
        dy = dot(spec[...], inv[0, :, :TILE])
        dyy = dot(spec[...], inv[0, :, TILE:])
        per = TILE // ny
        for s in range(per):
            w1 = recv[(i - steps) * per + s, 3].astype(f32)
            cols = slice(s * ny, (s + 1) * ny)
            for c in range(3):
                at = slice(c * rows, (c + 1) * rows)
                out[s, c] = (w1 * dy[at, cols] + viscosity * dyy[at, cols]).astype(bf16)


def y_part(recv, fwd, inv):
    parts, _, rows, ny = recv.shape
    n = parts * ny
    steps = n // TILE
    late = lambda i: jnp.maximum(i - steps, 0)
    return pl.pallas_call(
        functools.partial(y_kernel, steps),
        grid=(2 * steps,),
        in_specs=[full(recv.shape),
                  pl.BlockSpec((n, TILE), lambda i: (0, jnp.minimum(i, steps - 1))),
                  pl.BlockSpec((1, n, 2 * TILE), lambda i: (late(i), 0, 0))],
        out_specs=pl.BlockSpec((TILE // ny, 3, rows, ny), lambda i: (late(i), 0, 0, 0)),
        out_shape=jax.ShapeDtypeStruct((parts, 3, rows, ny), bf16),
        scratch_shapes=[pltpu.VMEM((3 * rows, n), bf16), pltpu.VMEM((3 * rows, n), bf16)],
        compiler_params=params(),
        cost_estimate=pl.CostEstimate(flops=6 * n * n * 3 * rows, bytes_accessed=8 * 1024 * 1024, transcendentals=0),
        name="y_part",
    )(recv, fwd, inv)


def join_kernel(count, scal, early, part, wind, cls_ref, drift, p0, p1, p2, q0, q1, q2, rhs, sums, acc):
    i = pl.program_id(0)

    @pl.when(i == 0)
    def _():
        acc[...] = jnp.zeros_like(acc)

    w = [wind[c].astype(f32) for c in range(3)]
    speed = jnp.sqrt(w[0] * w[0] + w[1] * w[1] + w[2] * w[2])
    slope = (0.5 * scal[1]) * w[2]
    total = jnp.zeros_like(speed)
    for c, (p, q) in enumerate(((p0, q0), (p1, q1), (p2, q2))):
        near, far = p[...].astype(f32), q[...].astype(f32)
        r = part[c] + drift[0, c].astype(f32) + slope * (near - far) + viscosity * (near + far)
        rhs[c] = r
        total += r * w[c]
    class_sums(scal[0] * speed * total, cls_ref[...], acc, count)

    @pl.when(i == pl.num_programs(0) - 1)
    def _():
        sums[...] = early[...] + to_lanes(acc, count, count)


def join(scal, early, part, wind, classes, drift, near, far, count):
    parts, _, rows, ny = drift.shape
    nx = parts * rows
    three = pl.BlockSpec((3, rows, ny), lambda i: (0, i, 0))
    plane = pl.BlockSpec((rows, ny), lambda i: (i, 0))
    return pl.pallas_call(
        functools.partial(join_kernel, count),
        grid=(parts,),
        in_specs=[SMEM, full((1, LANES)), three, three, plane,
                  pl.BlockSpec((1, 3, rows, ny), lambda i: (i, 0, 0, 0))] + [plane] * 6,
        out_specs=[three, full((1, LANES))],
        out_shape=[jax.ShapeDtypeStruct((3, nx, ny), f32), jax.ShapeDtypeStruct((1, LANES), f32)],
        scratch_shapes=[pltpu.VMEM((count, 8, ny), f32)],
        compiler_params=params(),
        cost_estimate=pl.CostEstimate(flops=100 * nx * ny, bytes_accessed=8 * 1024 * 1024, transcendentals=0),
        name="join",
    )(scal, early, part, wind, classes, drift, *near, *far)


def finish_kernel(count, scale, got, adj, rhs, new, sens):
    rows = got[...].reshape(-1, LANES)
    lane = lax.broadcasted_iota(jnp.int32, (1, LANES), 1)
    sums = jnp.sum(rows, axis=0, keepdims=True)
    tops = jnp.max(rows, axis=0, keepdims=True)
    top = jnp.max(jnp.where(lane == 2 * count, tops, 0.0), axis=1, keepdims=True)
    step = courant / (top + epsilon)
    for c in range(3):
        new[c] = adj[c] + step * rhs[c]

    @pl.when(pl.program_id(0) == 0)
    def _():
        later = pltpu.roll(sums, LANES - count, 1)
        sens[...] = -step * scale * (sums + step * later)


def finish(got, adj, rhs, count, scale):
    _, nx, ny = adj.shape
    parts = 4
    three = pl.BlockSpec((3, nx // parts, ny), lambda i: (0, i, 0))
    return pl.pallas_call(
        functools.partial(finish_kernel, count, scale),
        grid=(parts,),
        in_specs=[full(got.shape), three, three],
        out_specs=[three, full((1, LANES))],
        out_shape=[jax.ShapeDtypeStruct(adj.shape, f32), jax.ShapeDtypeStruct((1, LANES), f32)],
        compiler_params=params(),
        cost_estimate=pl.CostEstimate(flops=10 * nx * ny, bytes_accessed=5 * 1024 * 1024, transcendentals=0),
        name="finish",
    )(got, adj, rhs)


def swap(x, axes):
    return lax.all_to_all(x, axes, split_axis=0, concat_axis=0, tiled=True)


def local(adjoint, wind, classes, drag_coef):
    gz, gy = lax.axis_size("gz"), lax.axis_size("gy")
    _, _, nx, ny = adjoint.shape
    total_y = ny * gy
    count = drag_coef.shape[0]
    adj = adjoint.reshape(3, nx, ny)
    wnd = wind.reshape(3, nx, ny)

    fx, d1x, d2x = tables(nx)
    fy, d1y, d2y = tables(total_y)
    inv_x = np.concatenate([d1x.reshape(-1, TILE, nx), d2x.reshape(-1, TILE, nx)], axis=1)
    per = lambda d: d.reshape(-1, TILE, total_y).transpose(0, 2, 1)
    inv_y = np.concatenate([per(d1y), per(d2y)], axis=2)
    fwd_y = np.ascontiguousarray(fy.T)

    me = lax.axis_index("gz")
    height = jnp.exp(-2.0 * (me.astype(f32) + 0.5) / gz)
    sign = jnp.where(me % 2 == 0, 1.0, -1.0).astype(f32)
    scal = jnp.stack([height, sign])

    send, *lows = pack(adj, wnd, gy)
    recv = swap(send, "gy")

    pair = [(i, i ^ 1) for i in range(gz)]
    onward = [(i, i + 2) for i in range(0, gz - 2, 2)] + [(i, i - 2) for i in range(3, gz, 2)]
    near = [lax.ppermute(low, "gz", pair) for low in lows]
    far = [lax.ppermute(low, "gz", onward) for low in near]

    part, early = x_part(scal, drag_coef, jnp.asarray(fx), jnp.asarray(inv_x), lows, adj, wnd, classes)
    drift = swap(y_part(recv, jnp.asarray(fwd_y), jnp.asarray(inv_y)), "gy")
    rhs, sums = join(scal, early, part, wnd, classes, drift, near, far, count)

    everyone = gz * gy
    got = swap(jnp.broadcast_to(sums[None], (everyone, 1, LANES)), ("gz", "gy"))
    scale = 1.0 / math.sqrt(nx * total_y * gz / count)
    new, sens = finish(got, adj, rhs, count, scale)
    return new.reshape(adjoint.shape), sens[0, :count]


def solution(mesh):
    return jax.shard_map(
        local,
        mesh=mesh,
        in_specs=(P(None, "gz", None, "gy"), P(None, "gz", None, "gy"), P(None, "gy"), P()),
        out_specs=(P(None, "gz", None, "gy"), P()),
        check_vma=False,
    )
```

```python
import functools
import math

import jax
import jax.numpy as jnp
import ml_dtypes
import numpy as np
from jax import lax
from jax.experimental import pallas as pl
from jax.experimental.pallas import tpu as pltpu
from jax.sharding import PartitionSpec as P

viscosity = 0.3
courant = 0.8
epsilon = 1e-06
LANES = 128
TILE = 256
VMEM_MIB = 16
f32 = jnp.float32
bf16 = jnp.bfloat16


@functools.lru_cache(maxsize=None)
def tables(length):
    half = length // 2
    modes = np.arange(half)
    points = np.arange(length)
    angles = (2.0 * np.pi / length) * ((modes[:, None] * points[None, :]) % length)
    cosine, sine = np.cos(angles), np.sin(angles)
    forward = np.concatenate([cosine, -sine], axis=0)
    wave = (2.0 * np.pi / length) * modes
    weight = np.where(modes == 0, 1.0, 2.0) / length
    w1, w2 = (weight * wave)[:, None], (weight * wave * wave)[:, None]
    first = np.concatenate([-w1 * sine, -w1 * cosine], axis=0).T
    second = np.concatenate([-w2 * cosine, w2 * sine], axis=0).T
    low = lambda a: np.ascontiguousarray(a).astype(ml_dtypes.bfloat16)
    return low(forward), low(first), low(second)


@functools.lru_cache(maxsize=None)
def line_tables(length):
    half = length // 2
    modes = np.arange(half)
    angles = (2.0 * np.pi / length) * ((modes[:, None] * np.arange(length)[None, :]) % length)
    wave = (2.0 * np.pi / length) * modes
    weight = np.where(modes == 0, 1.0, 2.0) / length
    first = -(weight * wave) @ np.sin(angles)
    second = -(weight * wave * wave) @ np.cos(angles)
    gap = np.arange(half)[None, :] - np.arange(half)[:, None]
    made = []
    for row in (first, second):
        a, b = row[gap % length], row[(gap + half) % length]
        made += [0.5 * (a + b), 0.5 * (a - b)]
    every = np.stack(made).reshape(4, half, half // TILE, TILE).transpose(2, 0, 1, 3)
    return np.ascontiguousarray(every).astype(ml_dtypes.bfloat16)


CHUNKS = 4


def params(mib=VMEM_MIB, **more):
    return pltpu.CompilerParams(vmem_limit_bytes=mib * 1024 * 1024, **more)


def begin(copies, sems, first=0):
    made = [pltpu.make_async_copy(src, dst, sems.at[first + n]) for n, (src, dst) in enumerate(copies)]
    for copy in made:
        copy.start()
    return made


def finish_all(made):
    for copy in made:
        copy.wait()


def full(shape):
    return pl.BlockSpec(shape, lambda i: (0,) * len(shape))


SMEM = pl.BlockSpec(memory_space=pltpu.SMEM)
HBM = pl.BlockSpec(memory_space=pltpu.HBM)
SMALL = pl.BlockSpec(memory_space=pltpu.VMEM)
near_by = functools.partial(pltpu.with_memory_space_constraint, memory_space=pltpu.VMEM)
far_off = functools.partial(pltpu.with_memory_space_constraint, memory_space=pltpu.HBM)


def dot(a, b):
    return jnp.dot(a, b, preferred_element_type=f32)


def pack_kernel(adj, wind, send, lows, adj_v, wind_v, send_v, lows_v, sem_in, sem_out):
    parts, _, rows, _ = send.shape
    per = parts // CHUNKS
    loads, stores = [], []
    for k in range(CHUNKS):
        at = pl.ds(k * per * rows, per * rows)
        loads.append(begin([(adj.at[:, at], adj_v.at[:, at]), (wind.at[1, at], wind_v.at[at])], sem_in, 2 * k))
    for k in range(CHUNKS):
        finish_all(loads[k])
        for s in range(k * per, (k + 1) * per):
            at = slice(s * rows, (s + 1) * rows)
            for c in range(3):
                low = adj_v[c, at].astype(bf16)
                send_v[s, c] = low
                lows_v[c, at] = low
            send_v[s, 3] = wind_v[at]
        at, part = pl.ds(k * per * rows, per * rows), pl.ds(k * per, per)
        stores += begin([(send_v.at[part], send.at[part]), (lows_v.at[:, at], lows.at[:, at])], sem_out, 2 * k)
    finish_all(stores)


def pack(adj, wind, parts):
    _, nx, ny = adj.shape
    rows = nx // parts
    sent, kept = (parts, 4, rows, ny), (3, nx, ny)
    return pl.pallas_call(
        pack_kernel,
        in_specs=[HBM, HBM],
        out_specs=[HBM, HBM],
        out_shape=[pltpu.HBM(sent, bf16), pltpu.HBM(kept, bf16)],
        scratch_shapes=[pltpu.VMEM(kept, f32), pltpu.VMEM((nx, ny), bf16), pltpu.VMEM(sent, bf16), pltpu.VMEM(kept, bf16),
                        pltpu.SemaphoreType.DMA((2 * CHUNKS,)), pltpu.SemaphoreType.DMA((2 * CHUNKS,))],
        compiler_params=params(),
        cost_estimate=pl.CostEstimate(flops=0, bytes_accessed=nx * ny * 32, transcendentals=0),
        name="pack",
    )(far_off(adj), far_off(wind))


def class_sums(column, cls, acc, count):
    for k in range(count):
        kept = jnp.where(cls == k, column, 0.0)
        acc[k] += jnp.sum(kept.reshape(-1, 8, kept.shape[-1]), axis=0)


def to_lanes(acc, count, offset):
    per = jnp.sum(acc[...], axis=1)
    per = jnp.sum(per, axis=1, keepdims=True)
    row = lax.broadcasted_iota(jnp.int32, (count, LANES), 0)
    lane = lax.broadcasted_iota(jnp.int32, (count, LANES), 1)
    return jnp.sum(jnp.where(lane == row + offset, per, 0.0), axis=0, keepdims=True)


def x_kernel(steps, count, scal, coef, fwd, inv, lows, adj, wind, cls_ref, rhs, sums, low, spec, acc, top):
    i = pl.program_id(0)
    ny = lows.shape[2]

    @pl.when(i == 0)
    def _():
        for c in range(3):
            low[:, c * ny:(c + 1) * ny] = lows[c]
        acc[...] = jnp.zeros_like(acc)
        top[...] = jnp.zeros_like(top)

    @pl.when(i < steps)
    def _():
        spec[pl.ds(pl.multiple_of(i * TILE, TILE), TILE), :] = dot(fwd[...], low[...]).astype(bf16)

    @pl.when(i >= steps)
    def _():
        dx = dot(inv[0, :TILE], spec[...])
        dxx = dot(inv[0, TILE:], spec[...])
        cls = cls_ref[...]
        w = [wind[c].astype(f32) for c in range(3)]
        speed = jnp.sqrt(w[0] * w[0] + w[1] * w[1] + w[2] * w[2])
        weight = scal[0] * speed
        drag = jnp.zeros_like(speed)
        for k in range(count):
            drag = jnp.where(cls == k, coef[k], drag)
        damp = drag * weight + 2.0 * viscosity
        total = jnp.zeros_like(speed)
        for c in range(3):
            a = adj[c]
            total += a * w[c]
            cols = slice(c * ny, (c + 1) * ny)
            rhs[c] = w[0] * dx[:, cols] + viscosity * dxx[:, cols] - damp * a
        class_sums(weight * total, cls, acc, count)
        size = jnp.abs(w[0]) + jnp.abs(w[1]) + jnp.abs(w[2])
        top[...] = jnp.maximum(top[...], jnp.max(size.reshape(-1, 8, ny), axis=0))

    @pl.when(i == pl.num_programs(0) - 1)
    def _():
        lane = lax.broadcasted_iota(jnp.int32, (1, LANES), 1)
        peak = jnp.max(jnp.max(top[...], axis=0, keepdims=True), axis=1, keepdims=True)
        sums[...] = jnp.where(lane == 2 * count, peak, to_lanes(acc, count, 0))


def x_part(scal, coef, fwd, inv, lows, adj, wind, classes):
    _, nx, ny = adj.shape
    count = coef.shape[0]
    steps = nx // TILE
    late = lambda i: jnp.maximum(i - steps, 0)
    return pl.pallas_call(
        functools.partial(x_kernel, steps, count),
        grid=(2 * steps,),
        in_specs=[SMEM, SMEM,
                  pl.BlockSpec((TILE, nx), lambda i: (jnp.minimum(i, steps - 1), 0)),
                  pl.BlockSpec((1, 2 * TILE, nx), lambda i: (late(i), 0, 0))]
        + [full((3, nx, ny))]
        + [pl.BlockSpec((3, TILE, ny), lambda i: (0, late(i), 0)),
           pl.BlockSpec((3, TILE, ny), lambda i: (0, late(i), 0)),
           pl.BlockSpec((TILE, ny), lambda i: (late(i), 0))],
        out_specs=[pl.BlockSpec((3, TILE, ny), lambda i: (0, late(i), 0)), full((1, LANES))],
        out_shape=[pltpu.HBM((3, nx, ny), f32), jax.ShapeDtypeStruct((1, LANES), f32)],
        scratch_shapes=[pltpu.VMEM((nx, 3 * ny), bf16), pltpu.VMEM((nx, 3 * ny), bf16),
                        pltpu.VMEM((count, 8, ny), f32), pltpu.VMEM((8, ny), f32)],
        compiler_params=params(60, dimension_semantics=("arbitrary",)),
        cost_estimate=pl.CostEstimate(flops=6 * nx * nx * 3 * ny, bytes_accessed=12 * 1024 * 1024, transcendentals=0),
        name="x_part",
    )(scal, coef, fwd, inv, far_off(lows), adj, wind, classes)


def y_kernel(after, recv, table, out, plus, minus, table_v, out_v, sem_t, sem_o):
    parts, _, rows, ny = recv.shape
    half, steps = parts // 2, table.shape[0]
    tiles = begin([(table.at[t], table_v.at[t]) for t in range(steps)], sem_t)
    for s in range(half):
        for c in range(3):
            u, v = recv[s, c].astype(f32), recv[s + half, c].astype(f32)
            at = (slice(c * rows, (c + 1) * rows), slice(s * ny, (s + 1) * ny))
            plus[at] = (u + v).astype(bf16)
            minus[at] = (u - v).astype(bf16)
    per = TILE // ny
    stores = []
    for t in range(steps):
        tiles[t].wait()
        for c in range(3):
            at = slice(c * rows, (c + 1) * rows)
            p1, q1 = dot(plus[at], table_v[t, 0]), dot(minus[at], table_v[t, 1])
            p2, q2 = dot(plus[at], table_v[t, 2]), dot(minus[at], table_v[t, 3])
            for dy, dyy, base in ((p1 + q1, p2 + q2, t * per), (p1 - q1, p2 - q2, half + t * per)):
                for s in range(per):
                    cols = slice(s * ny, (s + 1) * ny)
                    w1 = recv[base + s, 3].astype(f32)
                    out_v[base + s, c] = (w1 * dy[:, cols] + viscosity * dyy[:, cols]).astype(bf16)
        ends = [pl.ds(base, per) for base in (t * per, half + t * per)]
        stores += begin([(out_v.at[e], out.at[e]) for e in ends], sem_o, 2 * t)
    finish_all(stores)


def y_part(after, recv, table):
    parts, _, rows, ny = recv.shape
    n, steps = parts * ny, table.shape[0]
    sent = (parts, 3, rows, ny)
    dma = pltpu.SemaphoreType.DMA
    return pl.pallas_call(
        y_kernel,
        in_specs=[SMALL, SMALL, HBM],
        out_specs=HBM,
        out_shape=pltpu.HBM(sent, bf16),
        scratch_shapes=[pltpu.VMEM((3 * rows, n // 2), bf16), pltpu.VMEM((3 * rows, n // 2), bf16),
                        pltpu.VMEM(table.shape, bf16), pltpu.VMEM(sent, bf16), dma((steps,)), dma((2 * steps,))],
        compiler_params=params(),
        cost_estimate=pl.CostEstimate(flops=2 * n * n * 3 * rows, bytes_accessed=4 * 1024 * 1024, transcendentals=0),
        name="y_part",
    )(after, near_by(recv), far_off(table))


def speed_of(w):
    return jnp.sqrt(w[0] * w[0] + w[1] * w[1] + w[2] * w[2])


def z_kernel(count, scal, early, part, wind, cls_ref, near, far, rhs, sums, acc):
    i = pl.program_id(0)

    @pl.when(i == 0)
    def _():
        acc[...] = jnp.zeros_like(acc)

    w = [wind[c].astype(f32) for c in range(3)]
    slope = (0.5 * scal[1]) * w[2]
    total = jnp.zeros_like(slope)
    for c in range(3):
        p, q = near[c].astype(f32), far[c].astype(f32)
        r = part[c] + slope * (p - q) + viscosity * (p + q)
        rhs[c] = r
        total += r * w[c]
    class_sums(scal[0] * speed_of(w) * total, cls_ref[...], acc, count)

    @pl.when(i == pl.num_programs(0) - 1)
    def _():
        sums[...] = early[...] + to_lanes(acc, count, count)


def z_part(scal, early, part, wind, classes, near, far, count):
    _, nx, ny = part.shape
    rows = nx // CHUNKS
    three = pl.BlockSpec((3, rows, ny), lambda i: (0, i, 0))
    return pl.pallas_call(
        functools.partial(z_kernel, count),
        grid=(CHUNKS,),
        in_specs=[SMEM, full((1, LANES)), three, three, pl.BlockSpec((rows, ny), lambda i: (i, 0)), three, three],
        out_specs=[three, full((1, LANES))],
        out_shape=[pltpu.HBM((3, nx, ny), f32), jax.ShapeDtypeStruct((1, LANES), f32)],
        scratch_shapes=[pltpu.VMEM((count, 8, ny), f32)],
        compiler_params=params(dimension_semantics=("arbitrary",)),
        cost_estimate=pl.CostEstimate(flops=100 * nx * ny, bytes_accessed=8 * 1024 * 1024, transcendentals=0),
        name="z_part",
    )(scal, early, far_off(part), far_off(wind), far_off(classes), far_off(near), far_off(far))


def join_kernel(count, scal, early, part, wind, classes, adj, drift, rhs, adj_v, sums,
                part_v, wind_v, cls_v, acc, sem_in, sem_adj):
    parts, _, rows, _ = drift.shape
    per = parts // CHUNKS
    loads = []
    for k in range(CHUNKS):
        at = pl.ds(k * per * rows, per * rows)
        loads.append(begin([(wind.at[:, at], wind_v.at[:, at]), (classes.at[at], cls_v.at[at]),
                            (part.at[:, at], part_v.at[:, at])], sem_in, 3 * k))
    kept = begin([(adj, adj_v)], sem_adj)
    acc[...] = jnp.zeros_like(acc)
    for k in range(CHUNKS):
        finish_all(loads[k])
        for s in range(k * per, (k + 1) * per):
            at = slice(s * rows, (s + 1) * rows)
            w = [wind_v[c, at].astype(f32) for c in range(3)]
            total = jnp.zeros_like(w[0])
            for c in range(3):
                d = drift[s, c].astype(f32)
                rhs[c, at] = part_v[c, at] + d
                total += d * w[c]
            class_sums(scal[0] * speed_of(w) * total, cls_v[at], acc, count)
    sums[...] = jnp.broadcast_to((early[...] + to_lanes(acc, count, count))[None], sums.shape)
    finish_all(kept)


def join(scal, early, part, wind, classes, adj, drift, count):
    parts, _, rows, ny = drift.shape
    nx = parts * rows
    whole = (3, nx, ny)
    dma = pltpu.SemaphoreType.DMA
    return pl.pallas_call(
        functools.partial(join_kernel, count),
        in_specs=[SMEM, SMALL, HBM, HBM, HBM, HBM, SMALL],
        out_specs=[SMALL, SMALL, SMALL],
        out_shape=[pltpu.VMEM(whole, f32), pltpu.VMEM(whole, f32), jax.ShapeDtypeStruct((parts, 1, LANES), f32)],
        scratch_shapes=[pltpu.VMEM(whole, f32), pltpu.VMEM(whole, bf16), pltpu.VMEM((nx, ny), jnp.int32),
                        pltpu.VMEM((count, 8, ny), f32), dma((3 * CHUNKS,)), dma((1,))],
        compiler_params=params(),
        cost_estimate=pl.CostEstimate(flops=100 * nx * ny, bytes_accessed=8 * 1024 * 1024, transcendentals=0),
        name="join",
    )(scal, early, far_off(part), far_off(wind), far_off(classes), far_off(adj), near_by(drift))


def merge(rows, count):
    lane = lax.broadcasted_iota(jnp.int32, (1, LANES), 1)
    return jnp.where(lane == 2 * count, jnp.max(rows, axis=0), jnp.sum(rows, axis=0))


def fold_kernel(count, got, out):
    out[...] = jnp.broadcast_to(merge(got[...], count)[None], out.shape)


def fold(got, size, count):
    return pl.pallas_call(
        functools.partial(fold_kernel, count),
        out_shape=jax.ShapeDtypeStruct((size, 1, LANES), f32),
        compiler_params=params(4),
        name="fold",
    )(got)


def finish_kernel(count, scale, got, adj, rhs, new, sens, new_v, sems):
    nx = adj.shape[1]
    rows = nx // CHUNKS
    sums = merge(got[...], count)
    lane = lax.broadcasted_iota(jnp.int32, (1, LANES), 1)
    top = jnp.max(jnp.where(lane == 2 * count, sums, 0.0), axis=1, keepdims=True)
    step = courant / (top + epsilon)
    stores = []
    for k in range(CHUNKS):
        at = slice(k * rows, (k + 1) * rows)
        for c in range(3):
            new_v[c, at] = adj[c, at] + step * rhs[c, at]
        at = pl.ds(k * rows, rows)
        stores += begin([(new_v.at[:, at], new.at[:, at])], sems, k)
    later = pltpu.roll(sums, LANES - count, 1)
    sens[...] = (-step * scale * (sums + step * later))[:, :count]
    finish_all(stores)


def finish(got, adj, rhs, count, scale):
    return pl.pallas_call(
        functools.partial(finish_kernel, count, scale),
        in_specs=[SMALL, SMALL, SMALL],
        out_specs=[HBM, SMALL],
        out_shape=[pltpu.HBM(adj.shape, f32), jax.ShapeDtypeStruct((1, count), f32)],
        scratch_shapes=[pltpu.VMEM(adj.shape, f32), pltpu.SemaphoreType.DMA((CHUNKS,))],
        compiler_params=params(),
        cost_estimate=pl.CostEstimate(flops=2 * adj.size, bytes_accessed=12 * adj.size, transcendentals=0),
        name="finish",
    )(got, near_by(adj), near_by(rhs))


def swap(x, axes):
    return lax.all_to_all(x, axes, split_axis=0, concat_axis=0, tiled=True)


def local(adjoint, wind, classes, drag_coef):
    gz, gy = lax.axis_size("gz"), lax.axis_size("gy")
    _, _, nx, ny = adjoint.shape
    total_y = ny * gy
    count = drag_coef.shape[0]
    adj = adjoint.reshape(3, nx, ny)
    wnd = wind.reshape(3, nx, ny)

    fx, d1x, d2x = tables(nx)
    inv_x = np.concatenate([d1x.reshape(-1, TILE, nx), d2x.reshape(-1, TILE, nx)], axis=1)

    me = lax.axis_index("gz")
    height = jnp.exp(-2.0 * (me.astype(f32) + 0.5) / gz)
    sign = jnp.where(me % 2 == 0, 1.0, -1.0).astype(f32)
    scal = jnp.stack([height, sign])

    send, lows = pack(adj, wnd, gy)
    recv = swap(send, "gy")

    pair = [(i, i ^ 1) for i in range(gz)]
    onward = [(i, i + 2) for i in range(0, gz - 2, 2)] + [(i, i - 2) for i in range(3, gz, 2)]
    near = lax.ppermute(lows, "gz", pair)
    far = lax.ppermute(near, "gz", onward)

    part, early = x_part(scal, drag_coef, jnp.asarray(fx), jnp.asarray(inv_x), lows, adj, wnd, classes)
    drift = swap(y_part(early, recv, jnp.asarray(line_tables(total_y))), "gy")
    part, early = z_part(scal, early, part, wnd, classes, near, far, count)
    rhs, adj, sums = join(scal, early, part, wnd, classes, adj, drift, count)

    got = swap(fold(swap(sums, "gy"), gz, count), "gz")
    scale = 1.0 / math.sqrt(nx * total_y * gz / count)
    new, sens = finish(got, adj, rhs, count, scale)
    return new.reshape(adjoint.shape), sens.reshape(count)


def solution(mesh):
    return jax.shard_map(
        local,
        mesh=mesh,
        in_specs=(P(None, "gz", None, "gy"), P(None, "gz", None, "gy"), P(None, "gy"), P()),
        out_specs=(P(None, "gz", None, "gy"), P()),
        check_vma=False,
    )
```

```python
import functools
import math

import jax
import jax.numpy as jnp
import ml_dtypes
import numpy as np
from jax import lax
from jax.experimental import pallas as pl
from jax.experimental.pallas import tpu as pltpu
from jax.sharding import PartitionSpec as P

viscosity = 0.3
courant = 0.8
epsilon = 1e-06
LANES = 128
TILE = 256
VMEM_MIB = 16
f32 = jnp.float32
bf16 = jnp.bfloat16


@functools.lru_cache(maxsize=None)
def tables(length):
    half = length // 2
    modes = np.arange(half)
    points = np.arange(length)
    angles = (2.0 * np.pi / length) * ((modes[:, None] * points[None, :]) % length)
    cosine, sine = np.cos(angles), np.sin(angles)
    forward = np.concatenate([cosine, -sine], axis=0)
    wave = (2.0 * np.pi / length) * modes
    weight = np.where(modes == 0, 1.0, 2.0) / length
    w1, w2 = (weight * wave)[:, None], (weight * wave * wave)[:, None]
    first = np.concatenate([-w1 * sine, -w1 * cosine], axis=0).T
    second = np.concatenate([-w2 * cosine, w2 * sine], axis=0).T
    low = lambda a: np.ascontiguousarray(a).astype(ml_dtypes.bfloat16)
    return low(forward), low(first), low(second)


@functools.lru_cache(maxsize=None)
def line_tables(length):
    half = length // 2
    modes = np.arange(half)
    angles = (2.0 * np.pi / length) * ((modes[:, None] * np.arange(length)[None, :]) % length)
    wave = (2.0 * np.pi / length) * modes
    weight = np.where(modes == 0, 1.0, 2.0) / length
    first = -(weight * wave) @ np.sin(angles)
    second = -(weight * wave * wave) @ np.cos(angles)
    gap = np.arange(half)[None, :] - np.arange(half)[:, None]
    made = []
    for row in (first, second):
        a, b = row[gap % length], row[(gap + half) % length]
        made += [0.5 * (a + b), 0.5 * (a - b)]
    every = np.stack(made).reshape(4, half, half // TILE, TILE).transpose(2, 0, 1, 3)
    return np.ascontiguousarray(every).astype(ml_dtypes.bfloat16)


CHUNKS = 4
GATE_FLOPS = 10**10


def params(mib=VMEM_MIB, **more):
    return pltpu.CompilerParams(vmem_limit_bytes=mib * 1024 * 1024, **more)


def begin(copies, sems, first=0):
    made = [pltpu.make_async_copy(src, dst, sems.at[first + n]) for n, (src, dst) in enumerate(copies)]
    for copy in made:
        copy.start()
    return made


def finish_all(made):
    for copy in made:
        copy.wait()


def full(shape):
    return pl.BlockSpec(shape, lambda i: (0,) * len(shape))


SMEM = pl.BlockSpec(memory_space=pltpu.SMEM)
HBM = pl.BlockSpec(memory_space=pltpu.HBM)
SMALL = pl.BlockSpec(memory_space=pltpu.VMEM)
near_by = functools.partial(pltpu.with_memory_space_constraint, memory_space=pltpu.VMEM)
far_off = functools.partial(pltpu.with_memory_space_constraint, memory_space=pltpu.HBM)


def dot(a, b):
    return jnp.dot(a, b, preferred_element_type=f32)


def pack_kernel(adj, wind, send, l0, l1, l2, adj_v, wind_v, send_v, lows_v, sem_in, sem_out):
    parts, _, rows, _ = send.shape
    per = parts // CHUNKS
    loads, stores = [], []
    for k in range(CHUNKS):
        at = pl.ds(k * per * rows, per * rows)
        loads.append(begin([(adj.at[:, at], adj_v.at[:, at]), (wind.at[1, at], wind_v.at[at])], sem_in, 2 * k))
    for k in range(CHUNKS):
        finish_all(loads[k])
        for s in range(k * per, (k + 1) * per):
            at = slice(s * rows, (s + 1) * rows)
            for c in range(3):
                low = adj_v[c, at].astype(bf16)
                send_v[s, c] = low
                lows_v[c, at] = low
            send_v[s, 3] = wind_v[at]
        at, part = pl.ds(k * per * rows, per * rows), pl.ds(k * per, per)
        stores += begin([(send_v.at[part], send.at[part])]
                        + [(lows_v.at[c, at], low.at[at]) for c, low in enumerate((l0, l1, l2))], sem_out, 4 * k)
    finish_all(stores)


def pack(adj, wind, parts):
    _, nx, ny = adj.shape
    rows = nx // parts
    sent, kept = (parts, 4, rows, ny), (3, nx, ny)
    return pl.pallas_call(
        pack_kernel,
        in_specs=[HBM, HBM],
        out_specs=[HBM] * 4,
        out_shape=[pltpu.HBM(sent, bf16)] + [pltpu.HBM((nx, ny), bf16)] * 3,
        scratch_shapes=[pltpu.VMEM(kept, f32), pltpu.VMEM((nx, ny), bf16), pltpu.VMEM(sent, bf16), pltpu.VMEM(kept, bf16),
                        pltpu.SemaphoreType.DMA((2 * CHUNKS,)), pltpu.SemaphoreType.DMA((4 * CHUNKS,))],
        compiler_params=params(),
        cost_estimate=pl.CostEstimate(flops=0, bytes_accessed=nx * ny * 32, transcendentals=0),
        name="pack",
    )(far_off(adj), far_off(wind))


def class_sums(column, cls, acc, count):
    for k in range(count):
        kept = jnp.where(cls == k, column, 0.0)
        acc[k] += jnp.sum(kept.reshape(-1, 8, kept.shape[-1]), axis=0)


def to_lanes(acc, count, offset):
    per = jnp.sum(acc[...], axis=1)
    per = jnp.sum(per, axis=1, keepdims=True)
    row = lax.broadcasted_iota(jnp.int32, (count, LANES), 0)
    lane = lax.broadcasted_iota(jnp.int32, (count, LANES), 1)
    return jnp.sum(jnp.where(lane == row + offset, per, 0.0), axis=0, keepdims=True)


def x_kernel(steps, count, scal, coef, fwd, inv, l0, l1, l2, adj, wind, cls_ref, rhs, sums, low, spec, acc, top):
    i = pl.program_id(0)
    ny = l0.shape[1]

    @pl.when(i == 0)
    def _():
        for c, ref in enumerate((l0, l1, l2)):
            low[:, c * ny:(c + 1) * ny] = ref[...]
        acc[...] = jnp.zeros_like(acc)
        top[...] = jnp.zeros_like(top)

    @pl.when(i < steps)
    def _():
        spec[pl.ds(pl.multiple_of(i * TILE, TILE), TILE), :] = dot(fwd[...], low[...]).astype(bf16)

    @pl.when(i >= steps)
    def _():
        dx = dot(inv[0, :TILE], spec[...])
        dxx = dot(inv[0, TILE:], spec[...])
        cls = cls_ref[...]
        w = [wind[c].astype(f32) for c in range(3)]
        speed = jnp.sqrt(w[0] * w[0] + w[1] * w[1] + w[2] * w[2])
        weight = scal[0] * speed
        drag = jnp.zeros_like(speed)
        for k in range(count):
            drag = jnp.where(cls == k, coef[k], drag)
        damp = drag * weight + 2.0 * viscosity
        total = jnp.zeros_like(speed)
        for c in range(3):
            a = adj[c]
            total += a * w[c]
            cols = slice(c * ny, (c + 1) * ny)
            rhs[c] = w[0] * dx[:, cols] + viscosity * dxx[:, cols] - damp * a
        class_sums(weight * total, cls, acc, count)
        size = jnp.abs(w[0]) + jnp.abs(w[1]) + jnp.abs(w[2])
        top[...] = jnp.maximum(top[...], jnp.max(size.reshape(-1, 8, ny), axis=0))

    @pl.when(i == pl.num_programs(0) - 1)
    def _():
        lane = lax.broadcasted_iota(jnp.int32, (1, LANES), 1)
        peak = jnp.max(jnp.max(top[...], axis=0, keepdims=True), axis=1, keepdims=True)
        sums[...] = jnp.where(lane == 2 * count, peak, to_lanes(acc, count, 0))


def x_part(scal, coef, fwd, inv, lows, adj, wind, classes):
    _, nx, ny = adj.shape
    count = coef.shape[0]
    steps = nx // TILE
    late = lambda i: jnp.maximum(i - steps, 0)
    return pl.pallas_call(
        functools.partial(x_kernel, steps, count),
        grid=(2 * steps,),
        in_specs=[SMEM, SMEM,
                  pl.BlockSpec((TILE, nx), lambda i: (jnp.minimum(i, steps - 1), 0)),
                  pl.BlockSpec((1, 2 * TILE, nx), lambda i: (late(i), 0, 0))]
        + [full((nx, ny))] * 3
        + [pl.BlockSpec((3, TILE, ny), lambda i: (0, late(i), 0)),
           pl.BlockSpec((3, TILE, ny), lambda i: (0, late(i), 0)),
           pl.BlockSpec((TILE, ny), lambda i: (late(i), 0))],
        out_specs=[pl.BlockSpec((3, TILE, ny), lambda i: (0, late(i), 0)), full((1, LANES))],
        out_shape=[pltpu.HBM((3, nx, ny), f32), pltpu.HBM((1, LANES), f32)],
        scratch_shapes=[pltpu.VMEM((nx, 3 * ny), bf16), pltpu.VMEM((nx, 3 * ny), bf16),
                        pltpu.VMEM((count, 8, ny), f32), pltpu.VMEM((8, ny), f32)],
        compiler_params=params(60, dimension_semantics=("arbitrary",)),
        cost_estimate=pl.CostEstimate(flops=6 * nx * nx * 3 * ny, bytes_accessed=12 * 1024 * 1024, transcendentals=0),
        name="x_part",
    )(scal, coef, fwd, inv, *[far_off(low) for low in lows], adj, wind, classes)


def y_kernel(after, recv, table, out, plus, minus, table_v, out_v, sem_t, sem_o):
    parts, _, rows, ny = recv.shape
    half, steps = parts // 2, table.shape[0]
    tiles = begin([(table.at[t], table_v.at[t]) for t in range(steps)], sem_t)
    for s in range(half):
        for c in range(3):
            u, v = recv[s, c].astype(f32), recv[s + half, c].astype(f32)
            at = (slice(c * rows, (c + 1) * rows), slice(s * ny, (s + 1) * ny))
            plus[at] = (u + v).astype(bf16)
            minus[at] = (u - v).astype(bf16)
    per = TILE // ny
    stores = []
    for t in range(steps):
        tiles[t].wait()
        for c in range(3):
            at = slice(c * rows, (c + 1) * rows)
            p1, q1 = dot(plus[at], table_v[t, 0]), dot(minus[at], table_v[t, 1])
            p2, q2 = dot(plus[at], table_v[t, 2]), dot(minus[at], table_v[t, 3])
            for dy, dyy, base in ((p1 + q1, p2 + q2, t * per), (p1 - q1, p2 - q2, half + t * per)):
                for s in range(per):
                    cols = slice(s * ny, (s + 1) * ny)
                    w1 = recv[base + s, 3].astype(f32)
                    out_v[base + s, c] = (w1 * dy[:, cols] + viscosity * dyy[:, cols]).astype(bf16)
        ends = [pl.ds(base, per) for base in (t * per, half + t * per)]
        stores += begin([(out_v.at[e], out.at[e]) for e in ends], sem_o, 2 * t)
    finish_all(stores)


def y_part(after, recv, table):
    parts, _, rows, ny = recv.shape
    n, steps = parts * ny, table.shape[0]
    sent = (parts, 3, rows, ny)
    dma = pltpu.SemaphoreType.DMA
    return pl.pallas_call(
        y_kernel,
        in_specs=[HBM, SMALL, HBM],
        out_specs=HBM,
        out_shape=pltpu.HBM(sent, bf16),
        scratch_shapes=[pltpu.VMEM((3 * rows, n // 2), bf16), pltpu.VMEM((3 * rows, n // 2), bf16),
                        pltpu.VMEM(table.shape, bf16), pltpu.VMEM(sent, bf16), dma((steps,)), dma((2 * steps,))],
        compiler_params=params(),
        cost_estimate=pl.CostEstimate(flops=2 * n * n * 3 * rows, bytes_accessed=4 * 1024 * 1024, transcendentals=0),
        name="y_part",
    )(far_off(after), near_by(recv), far_off(table))


def speed_of(w):
    return jnp.sqrt(w[0] * w[0] + w[1] * w[1] + w[2] * w[2])


def gate_kernel(early, q0, q1, q2, out):
    out[...] = early[...]


def gate(early, far):
    return pl.pallas_call(
        gate_kernel,
        in_specs=[SMALL, HBM, HBM, HBM],
        out_specs=SMALL,
        out_shape=jax.ShapeDtypeStruct(early.shape, f32),
        compiler_params=params(4),
        cost_estimate=pl.CostEstimate(flops=GATE_FLOPS, bytes_accessed=1024, transcendentals=0),
        name="gate",
    )(early, *[far_off(q) for q in far])


def join_kernel(count, scal, early, part, wind, classes, adj, p0, p1, p2, q0, q1, q2, drift, rhs, adj_v, sums,
                part_v, wind_v, cls_v, near_v, far_v, acc, sem_in, sem_adj):
    parts, _, rows, _ = drift.shape
    per = parts // CHUNKS
    loads = []
    for k in range(CHUNKS):
        at = pl.ds(k * per * rows, per * rows)
        loads.append(begin([(wind.at[:, at], wind_v.at[:, at]), (classes.at[at], cls_v.at[at]),
                            (part.at[:, at], part_v.at[:, at])]
                           + [(p.at[at], near_v.at[c, at]) for c, p in enumerate((p0, p1, p2))]
                           + [(q.at[at], far_v.at[c, at]) for c, q in enumerate((q0, q1, q2))], sem_in, 9 * k))
    kept = begin([(adj, adj_v)], sem_adj)
    acc[...] = jnp.zeros_like(acc)
    for k in range(CHUNKS):
        finish_all(loads[k])
        for s in range(k * per, (k + 1) * per):
            at = slice(s * rows, (s + 1) * rows)
            w = [wind_v[c, at].astype(f32) for c in range(3)]
            slope = (0.5 * scal[1]) * w[2]
            up, down = viscosity + slope, viscosity - slope
            total = jnp.zeros_like(slope)
            for c in range(3):
                r = part_v[c, at] + drift[s, c].astype(f32)
                r += up * near_v[c, at].astype(f32) + down * far_v[c, at].astype(f32)
                rhs[c, at] = r
                total += r * w[c]
            class_sums(scal[0] * speed_of(w) * total, cls_v[at], acc, count)
    sums[...] = jnp.broadcast_to((early[...] + to_lanes(acc, count, count))[None], sums.shape)
    finish_all(kept)


def join(scal, early, part, wind, classes, adj, near, far, drift, count):
    parts, _, rows, ny = drift.shape
    nx = parts * rows
    whole = (3, nx, ny)
    dma = pltpu.SemaphoreType.DMA
    return pl.pallas_call(
        functools.partial(join_kernel, count),
        in_specs=[SMEM, SMALL] + [HBM] * 10 + [SMALL],
        out_specs=[SMALL, SMALL, SMALL],
        out_shape=[pltpu.VMEM(whole, f32), pltpu.VMEM(whole, f32), jax.ShapeDtypeStruct((parts, 1, LANES), f32)],
        scratch_shapes=[pltpu.VMEM(whole, f32), pltpu.VMEM(whole, bf16), pltpu.VMEM((nx, ny), jnp.int32),
                        pltpu.VMEM(whole, bf16), pltpu.VMEM(whole, bf16),
                        pltpu.VMEM((count, 8, ny), f32), dma((9 * CHUNKS,)), dma((1,))],
        compiler_params=params(),
        cost_estimate=pl.CostEstimate(flops=100 * nx * ny, bytes_accessed=8 * 1024 * 1024, transcendentals=0),
        name="join",
    )(scal, early, far_off(part), far_off(wind), far_off(classes), far_off(adj),
      *[far_off(a) for a in near + far], near_by(drift))


def merge(rows, count):
    lane = lax.broadcasted_iota(jnp.int32, (1, LANES), 1)
    return jnp.where(lane == 2 * count, jnp.max(rows, axis=0), jnp.sum(rows, axis=0))


def fold_kernel(count, got, out):
    out[...] = jnp.broadcast_to(merge(got[...], count)[None], out.shape)


def fold(got, size, count):
    return pl.pallas_call(
        functools.partial(fold_kernel, count),
        out_shape=jax.ShapeDtypeStruct((size, 1, LANES), f32),
        compiler_params=params(4),
        name="fold",
    )(got)


def finish_kernel(count, scale, got, adj, rhs, new, sens, new_v, sems):
    nx = adj.shape[1]
    rows = nx // CHUNKS
    sums = merge(got[...], count)
    lane = lax.broadcasted_iota(jnp.int32, (1, LANES), 1)
    top = jnp.max(jnp.where(lane == 2 * count, sums, 0.0), axis=1, keepdims=True)
    step = courant / (top + epsilon)
    stores = []
    for k in range(CHUNKS):
        at = slice(k * rows, (k + 1) * rows)
        for c in range(3):
            new_v[c, at] = adj[c, at] + step * rhs[c, at]
        at = pl.ds(k * rows, rows)
        stores += begin([(new_v.at[:, at], new.at[:, at])], sems, k)
    later = pltpu.roll(sums, LANES - count, 1)
    sens[...] = (-step * scale * (sums + step * later))[:, :count]
    finish_all(stores)


def finish(got, adj, rhs, count, scale):
    return pl.pallas_call(
        functools.partial(finish_kernel, count, scale),
        in_specs=[SMALL, SMALL, SMALL],
        out_specs=[HBM, SMALL],
        out_shape=[pltpu.HBM(adj.shape, f32), jax.ShapeDtypeStruct((1, count), f32)],
        scratch_shapes=[pltpu.VMEM(adj.shape, f32), pltpu.SemaphoreType.DMA((CHUNKS,))],
        compiler_params=params(),
        cost_estimate=pl.CostEstimate(flops=2 * adj.size, bytes_accessed=12 * adj.size, transcendentals=0),
        name="finish",
    )(got, near_by(adj), near_by(rhs))


def swap(x, axes):
    return lax.all_to_all(x, axes, split_axis=0, concat_axis=0, tiled=True)


def local(adjoint, wind, classes, drag_coef):
    gz, gy = lax.axis_size("gz"), lax.axis_size("gy")
    _, _, nx, ny = adjoint.shape
    total_y = ny * gy
    count = drag_coef.shape[0]
    adj = adjoint.reshape(3, nx, ny)
    wnd = wind.reshape(3, nx, ny)

    fx, d1x, d2x = tables(nx)
    inv_x = np.concatenate([d1x.reshape(-1, TILE, nx), d2x.reshape(-1, TILE, nx)], axis=1)

    me = lax.axis_index("gz")
    height = jnp.exp(-2.0 * (me.astype(f32) + 0.5) / gz)
    sign = jnp.where(me % 2 == 0, 1.0, -1.0).astype(f32)
    scal = jnp.stack([height, sign])

    send, *lows = pack(adj, wnd, gy)
    recv = swap(send, "gy")

    pair = [(i, i ^ 1) for i in range(gz)]
    onward = [(i, i + 2) for i in range(0, gz - 2, 2)] + [(i, i - 2) for i in range(3, gz, 2)]
    near = [lax.ppermute(low, "gz", pair) for low in lows]
    far = [lax.ppermute(low, "gz", onward) for low in near]

    part, early = x_part(scal, drag_coef, jnp.asarray(fx), jnp.asarray(inv_x), lows, adj, wnd, classes)
    drift = swap(y_part(early, recv, jnp.asarray(line_tables(total_y))), "gy")
    rhs, adj, sums = join(scal, gate(early, far), part, wnd, classes, adj, near, far, drift, count)

    got = swap(fold(swap(sums, "gy"), gz, count), "gz")
    scale = 1.0 / math.sqrt(nx * total_y * gz / count)
    new, sens = finish(got, adj, rhs, count, scale)
    return new.reshape(adjoint.shape), sens.reshape(count)


def solution(mesh):
    return jax.shard_map(
        local,
        mesh=mesh,
        in_specs=(P(None, "gz", None, "gy"), P(None, "gz", None, "gy"), P(None, "gy"), P()),
        out_specs=(P(None, "gz", None, "gy"), P()),
        check_vma=False,
    )
```

```python
import functools
import math

import jax
import jax.numpy as jnp
import ml_dtypes
import numpy as np
from jax import lax
from jax.experimental import pallas as pl
from jax.experimental.pallas import tpu as pltpu
from jax.sharding import PartitionSpec as P

viscosity = 0.3
courant = 0.8
epsilon = 1e-06
LANES = 128
TILE = 256
VMEM_MIB = 16
f32 = jnp.float32
bf16 = jnp.bfloat16


@functools.lru_cache(maxsize=None)
def tables(length):
    half = length // 2
    modes = np.arange(half)
    points = np.arange(length)
    angles = (2.0 * np.pi / length) * ((modes[:, None] * points[None, :]) % length)
    cosine, sine = np.cos(angles), np.sin(angles)
    forward = np.concatenate([cosine, -sine], axis=0)
    wave = (2.0 * np.pi / length) * modes
    weight = np.where(modes == 0, 1.0, 2.0) / length
    w1, w2 = (weight * wave)[:, None], (weight * wave * wave)[:, None]
    first = np.concatenate([-w1 * sine, -w1 * cosine], axis=0).T
    second = np.concatenate([-w2 * cosine, w2 * sine], axis=0).T
    low = lambda a: np.ascontiguousarray(a).astype(ml_dtypes.bfloat16)
    return low(forward), low(first), low(second)


@functools.lru_cache(maxsize=None)
def line_tables(length):
    half = length // 2
    modes = np.arange(half)
    angles = (2.0 * np.pi / length) * ((modes[:, None] * np.arange(length)[None, :]) % length)
    wave = (2.0 * np.pi / length) * modes
    weight = np.where(modes == 0, 1.0, 2.0) / length
    first = -(weight * wave) @ np.sin(angles)
    second = -(weight * wave * wave) @ np.cos(angles)
    gap = np.arange(half)[None, :] - np.arange(half)[:, None]
    made = []
    for row in (first, second):
        a, b = row[gap % length], row[(gap + half) % length]
        made += [0.5 * (a + b), 0.5 * (a - b)]
    every = np.stack(made).reshape(4, half, half // TILE, TILE).transpose(2, 0, 1, 3)
    return np.ascontiguousarray(every).astype(ml_dtypes.bfloat16)


CHUNKS = 4
GATE_FLOPS = 10**10


def params(mib=VMEM_MIB, **more):
    return pltpu.CompilerParams(vmem_limit_bytes=mib * 1024 * 1024, **more)


def begin(copies, sems, first=0):
    made = [pltpu.make_async_copy(src, dst, sems.at[first + n]) for n, (src, dst) in enumerate(copies)]
    for copy in made:
        copy.start()
    return made


def finish_all(made):
    for copy in made:
        copy.wait()


def full(shape):
    return pl.BlockSpec(shape, lambda i: (0,) * len(shape))


SMEM = pl.BlockSpec(memory_space=pltpu.SMEM)
HBM = pl.BlockSpec(memory_space=pltpu.HBM)
SMALL = pl.BlockSpec(memory_space=pltpu.VMEM)
near_by = functools.partial(pltpu.with_memory_space_constraint, memory_space=pltpu.VMEM)
far_off = functools.partial(pltpu.with_memory_space_constraint, memory_space=pltpu.HBM)


def dot(a, b):
    return jnp.dot(a, b, preferred_element_type=f32)


def pack_kernel(adj, wind, send, l0, l1, l2, adj_v, wind_v, send_v, lows_v, sem_in, sem_out):
    parts, _, rows, _ = send.shape
    per = parts // CHUNKS
    loads, stores = [], []
    for k in range(CHUNKS):
        at = pl.ds(k * per * rows, per * rows)
        loads.append(begin([(adj.at[:, at], adj_v.at[:, at]), (wind.at[1, at], wind_v.at[at])], sem_in, 2 * k))
    for k in range(CHUNKS):
        finish_all(loads[k])
        for s in range(k * per, (k + 1) * per):
            at = slice(s * rows, (s + 1) * rows)
            for c in range(3):
                low = adj_v[c, at].astype(bf16)
                send_v[s, c] = low
                lows_v[c, at] = low
            send_v[s, 3] = wind_v[at]
        at, part = pl.ds(k * per * rows, per * rows), pl.ds(k * per, per)
        stores += begin([(send_v.at[part], send.at[part])]
                        + [(lows_v.at[c, at], low.at[at]) for c, low in enumerate((l0, l1, l2))], sem_out, 4 * k)
    finish_all(stores)


def pack(adj, wind, parts):
    _, nx, ny = adj.shape
    rows = nx // parts
    sent, kept = (parts, 4, rows, ny), (3, nx, ny)
    return pl.pallas_call(
        pack_kernel,
        in_specs=[HBM, HBM],
        out_specs=[HBM] * 4,
        out_shape=[pltpu.HBM(sent, bf16)] + [pltpu.HBM((nx, ny), bf16)] * 3,
        scratch_shapes=[pltpu.VMEM(kept, f32), pltpu.VMEM((nx, ny), bf16), pltpu.VMEM(sent, bf16), pltpu.VMEM(kept, bf16),
                        pltpu.SemaphoreType.DMA((2 * CHUNKS,)), pltpu.SemaphoreType.DMA((4 * CHUNKS,))],
        compiler_params=params(),
        cost_estimate=pl.CostEstimate(flops=0, bytes_accessed=nx * ny * 32, transcendentals=0),
        name="pack",
    )(far_off(adj), far_off(wind))


def speed_of(w):
    return jnp.sqrt(w[0] * w[0] + w[1] * w[1] + w[2] * w[2])


def class_sums(column, cls, acc, count):
    for k in range(count):
        kept = jnp.where(cls == k, column, 0.0)
        acc[k] += jnp.sum(kept.reshape(-1, 8, kept.shape[-1]), axis=0)


def to_lanes(acc, count, offset):
    per = jnp.sum(acc[...], axis=1)
    per = jnp.sum(per, axis=1, keepdims=True)
    row = lax.broadcasted_iota(jnp.int32, (count, LANES), 0)
    lane = lax.broadcasted_iota(jnp.int32, (count, LANES), 1)
    return jnp.sum(jnp.where(lane == row + offset, per, 0.0), axis=0, keepdims=True)


def x_kernel(count, scal, coef, fwd, inv, l0, l1, l2, adj, wind, classes, rhs, sums,
             low, spec, fwd_v, inv_v, adj_v, wind_v, cls_v, rhs_v, acc, top, sem_l, sem_f, sem_i, sem_o):
    nx, ny = l0.shape
    steps = nx // TILE
    ats = [pl.ds(t * TILE, TILE) for t in range(steps)]
    lines = begin([(ref, low.at[:, pl.ds(c * ny, ny)]) for c, ref in enumerate((l0, l1, l2))], sem_l)
    tiles = begin([(fwd.at[at], fwd_v.at[at]) for at in ats], sem_f)
    loads = [begin([(inv.at[t], inv_v.at[t]), (adj.at[:, at], adj_v.at[:, at]), (wind.at[:, at], wind_v.at[:, at]),
                    (classes.at[at], cls_v.at[at])], sem_i, 4 * t) for t, at in enumerate(ats)]
    acc[...] = jnp.zeros_like(acc)
    top[...] = jnp.zeros_like(top)
    finish_all(lines)
    for t in range(0, steps, 2):
        finish_all(tiles[t:t + 2])
        at = slice(t * TILE, (t + 2) * TILE)
        spec[at] = dot(fwd_v[at], low[...]).astype(bf16)
    stores = []
    for t, at in enumerate(ats):
        finish_all(loads[t])
        both = dot(inv_v[t], spec[...])
        dx, dxx = both[:TILE], both[TILE:]
        cls = cls_v[at]
        w = [wind_v[c, at].astype(f32) for c in range(3)]
        speed = speed_of(w)
        weight = scal[0] * speed
        drag = jnp.zeros_like(speed)
        for k in range(count):
            drag = jnp.where(cls == k, coef[k], drag)
        damp = drag * weight + 2.0 * viscosity
        total = jnp.zeros_like(speed)
        for c in range(3):
            a = adj_v[c, at]
            total += a * w[c]
            cols = slice(c * ny, (c + 1) * ny)
            rhs_v[c, at] = w[0] * dx[:, cols] + viscosity * dxx[:, cols] - damp * a
        stores += begin([(rhs_v.at[:, at], rhs.at[:, at])], sem_o, t)
        class_sums(weight * total, cls, acc, count)
        size = jnp.abs(w[0]) + jnp.abs(w[1]) + jnp.abs(w[2])
        top[...] = jnp.maximum(top[...], jnp.max(size.reshape(-1, 8, ny), axis=0))
    lane = lax.broadcasted_iota(jnp.int32, (1, LANES), 1)
    peak = jnp.max(jnp.max(top[...], axis=0, keepdims=True), axis=1, keepdims=True)
    sums[...] = jnp.where(lane == 2 * count, peak, to_lanes(acc, count, 0))
    finish_all(stores)


def x_part(scal, coef, fwd, inv, lows, adj, wind, classes):
    _, nx, ny = adj.shape
    count = coef.shape[0]
    steps = nx // TILE
    dma = pltpu.SemaphoreType.DMA
    return pl.pallas_call(
        functools.partial(x_kernel, count),
        in_specs=[SMEM, SMEM] + [HBM] * 8,
        out_specs=[HBM, SMALL],
        out_shape=[pltpu.HBM((3, nx, ny), f32), jax.ShapeDtypeStruct((1, LANES), f32)],
        scratch_shapes=[pltpu.VMEM((nx, 3 * ny), bf16), pltpu.VMEM((nx, 3 * ny), bf16),
                        pltpu.VMEM(fwd.shape, bf16), pltpu.VMEM(inv.shape, bf16),
                        pltpu.VMEM(adj.shape, f32), pltpu.VMEM(adj.shape, bf16), pltpu.VMEM((nx, ny), jnp.int32),
                        pltpu.VMEM(adj.shape, f32), pltpu.VMEM((count, 8, ny), f32), pltpu.VMEM((8, ny), f32),
                        dma((3,)), dma((steps,)), dma((4 * steps,)), dma((steps,))],
        compiler_params=params(32),
        cost_estimate=pl.CostEstimate(flops=6 * nx * nx * 3 * ny, bytes_accessed=12 * 1024 * 1024, transcendentals=0),
        name="x_part",
    )(scal, coef, far_off(fwd), far_off(inv), *[far_off(low) for low in lows], far_off(adj), far_off(wind),
      far_off(classes))


def y_kernel(after, recv, table, out, plus, minus, table_v, out_v, sem_t, sem_o):
    parts, _, rows, ny = recv.shape
    half, steps = parts // 2, table.shape[0]
    tiles = begin([(table.at[t], table_v.at[t]) for t in range(steps)], sem_t)
    for s in range(half):
        for c in range(3):
            u, v = recv[s, c].astype(f32), recv[s + half, c].astype(f32)
            at = (slice(c * rows, (c + 1) * rows), slice(s * ny, (s + 1) * ny))
            plus[at] = (u + v).astype(bf16)
            minus[at] = (u - v).astype(bf16)
    per = TILE // ny
    stores = []
    for t in range(steps):
        tiles[t].wait()
        for c in range(3):
            at = slice(c * rows, (c + 1) * rows)
            p1, q1 = dot(plus[at], table_v[t, 0]), dot(minus[at], table_v[t, 1])
            p2, q2 = dot(plus[at], table_v[t, 2]), dot(minus[at], table_v[t, 3])
            for dy, dyy, base in ((p1 + q1, p2 + q2, t * per), (p1 - q1, p2 - q2, half + t * per)):
                for s in range(per):
                    cols = slice(s * ny, (s + 1) * ny)
                    w1 = recv[base + s, 3].astype(f32)
                    out_v[base + s, c] = (w1 * dy[:, cols] + viscosity * dyy[:, cols]).astype(bf16)
        ends = [pl.ds(base, per) for base in (t * per, half + t * per)]
        stores += begin([(out_v.at[e], out.at[e]) for e in ends], sem_o, 2 * t)
    finish_all(stores)


def y_part(after, recv, table):
    parts, _, rows, ny = recv.shape
    n, steps = parts * ny, table.shape[0]
    sent = (parts, 3, rows, ny)
    dma = pltpu.SemaphoreType.DMA
    return pl.pallas_call(
        y_kernel,
        in_specs=[HBM, SMALL, HBM],
        out_specs=HBM,
        out_shape=pltpu.HBM(sent, bf16),
        scratch_shapes=[pltpu.VMEM((3 * rows, n // 2), bf16), pltpu.VMEM((3 * rows, n // 2), bf16),
                        pltpu.VMEM(table.shape, bf16), pltpu.VMEM(sent, bf16), dma((steps,)), dma((2 * steps,))],
        compiler_params=params(),
        cost_estimate=pl.CostEstimate(flops=2 * n * n * 3 * rows, bytes_accessed=4 * 1024 * 1024, transcendentals=0),
        name="y_part",
    )(far_off(after), near_by(recv), far_off(table))


def gate_kernel(early, q0, q1, q2, out):
    out[...] = early[...]


def gate(early, far):
    return pl.pallas_call(
        gate_kernel,
        in_specs=[SMALL, HBM, HBM, SMALL],
        out_specs=SMALL,
        out_shape=jax.ShapeDtypeStruct(early.shape, f32),
        compiler_params=params(4),
        cost_estimate=pl.CostEstimate(flops=GATE_FLOPS, bytes_accessed=1024, transcendentals=0),
        name="gate",
    )(early, *[far_off(q) for q in far[:2]], near_by(far[2]))


def join_kernel(count, scal, early, part, wind, classes, adj, p0, p1, p2, q0, q1, q2, drift, rhs, adj_v, sums,
                part_v, wind_v, cls_v, near_v, far_v, acc, sem_in, sem_adj):
    parts, _, rows, _ = drift.shape
    per = parts // CHUNKS
    loads = []
    for k in range(CHUNKS):
        at = pl.ds(k * per * rows, per * rows)
        loads.append(begin([(wind.at[:, at], wind_v.at[:, at]), (classes.at[at], cls_v.at[at]),
                            (part.at[:, at], part_v.at[:, at])]
                           + [(p.at[at], near_v.at[c, at]) for c, p in enumerate((p0, p1, p2))]
                           + [(q.at[at], far_v.at[c, at]) for c, q in enumerate((q0, q1))], sem_in, 8 * k))
    kept = begin([(adj, adj_v)], sem_adj)
    acc[...] = jnp.zeros_like(acc)
    for k in range(CHUNKS):
        finish_all(loads[k])
        for s in range(k * per, (k + 1) * per):
            at = slice(s * rows, (s + 1) * rows)
            w = [wind_v[c, at].astype(f32) for c in range(3)]
            slope = (0.5 * scal[1]) * w[2]
            up, down = viscosity + slope, viscosity - slope
            total = jnp.zeros_like(slope)
            for c in range(3):
                q = q2[at] if c == 2 else far_v[c, at]
                r = part_v[c, at] + drift[s, c].astype(f32)
                r += up * near_v[c, at].astype(f32) + down * q.astype(f32)
                rhs[c, at] = r
                total += r * w[c]
            class_sums(scal[0] * speed_of(w) * total, cls_v[at], acc, count)
    sums[...] = jnp.broadcast_to((early[...] + to_lanes(acc, count, count))[None], sums.shape)
    finish_all(kept)


def join(scal, early, part, wind, classes, adj, near, far, drift, count):
    parts, _, rows, ny = drift.shape
    nx = parts * rows
    whole = (3, nx, ny)
    dma = pltpu.SemaphoreType.DMA
    return pl.pallas_call(
        functools.partial(join_kernel, count),
        in_specs=[SMEM, SMALL] + [HBM] * 9 + [SMALL] * 2,
        out_specs=[SMALL, SMALL, SMALL],
        out_shape=[pltpu.VMEM(whole, f32), pltpu.VMEM(whole, f32), jax.ShapeDtypeStruct((2 * parts, 1, LANES), f32)],
        scratch_shapes=[pltpu.VMEM(whole, f32), pltpu.VMEM(whole, bf16), pltpu.VMEM((nx, ny), jnp.int32),
                        pltpu.VMEM(whole, bf16), pltpu.VMEM((2, nx, ny), bf16),
                        pltpu.VMEM((count, 8, ny), f32), dma((8 * CHUNKS,)), dma((1,))],
        compiler_params=params(),
        cost_estimate=pl.CostEstimate(flops=100 * nx * ny, bytes_accessed=8 * 1024 * 1024, transcendentals=0),
        name="join",
    )(scal, early, far_off(part), far_off(wind), far_off(classes), far_off(adj),
      *[far_off(a) for a in near + far[:2]], near_by(far[2]), near_by(drift))


def merge(rows, count):
    lane = lax.broadcasted_iota(jnp.int32, (1, LANES), 1)
    return jnp.where(lane == 2 * count, jnp.max(rows, axis=0), jnp.sum(rows, axis=0))


def fold_kernel(count, got, out):
    out[...] = jnp.broadcast_to(merge(got[...], count)[None], out.shape)


def fold(got, size, count):
    return pl.pallas_call(
        functools.partial(fold_kernel, count),
        out_shape=jax.ShapeDtypeStruct((size, 1, LANES), f32),
        compiler_params=params(4),
        name="fold",
    )(got)


def finish_kernel(count, scale, got, adj, rhs, new, sens, new_v, sems):
    nx = adj.shape[1]
    rows = nx // CHUNKS
    sums = merge(got[...], count)
    lane = lax.broadcasted_iota(jnp.int32, (1, LANES), 1)
    top = jnp.max(jnp.where(lane == 2 * count, sums, 0.0), axis=1, keepdims=True)
    step = courant / (top + epsilon)
    stores = []
    for k in range(CHUNKS):
        at = slice(k * rows, (k + 1) * rows)
        for c in range(3):
            new_v[c, at] = adj[c, at] + step * rhs[c, at]
        at = pl.ds(k * rows, rows)
        stores += begin([(new_v.at[:, at], new.at[:, at])], sems, k)
    later = pltpu.roll(sums, LANES - count, 1)
    sens[...] = (-step * scale * (sums + step * later))[:, :count]
    finish_all(stores)


def finish(got, adj, rhs, count, scale):
    return pl.pallas_call(
        functools.partial(finish_kernel, count, scale),
        in_specs=[SMALL, SMALL, SMALL],
        out_specs=[HBM, SMALL],
        out_shape=[pltpu.HBM(adj.shape, f32), jax.ShapeDtypeStruct((1, count), f32)],
        scratch_shapes=[pltpu.VMEM(adj.shape, f32), pltpu.SemaphoreType.DMA((CHUNKS,))],
        compiler_params=params(),
        cost_estimate=pl.CostEstimate(flops=2 * adj.size, bytes_accessed=12 * adj.size, transcendentals=0),
        name="finish",
    )(got, near_by(adj), near_by(rhs))


def swap(x, axes, groups=None):
    return lax.all_to_all(x, axes, split_axis=0, concat_axis=0, axis_index_groups=groups, tiled=True)


def local(adjoint, wind, classes, drag_coef):
    gz, gy = lax.axis_size("gz"), lax.axis_size("gy")
    _, _, nx, ny = adjoint.shape
    total_y = ny * gy
    count = drag_coef.shape[0]
    adj = adjoint.reshape(3, nx, ny)
    wnd = wind.reshape(3, nx, ny)

    fx, d1x, d2x = tables(nx)
    inv_x = np.concatenate([d1x.reshape(-1, TILE, nx), d2x.reshape(-1, TILE, nx)], axis=1)

    me = lax.axis_index("gz")
    height = jnp.exp(-2.0 * (me.astype(f32) + 0.5) / gz)
    sign = jnp.where(me % 2 == 0, 1.0, -1.0).astype(f32)
    scal = jnp.stack([height, sign])

    send, *lows = pack(adj, wnd, gy)
    recv = swap(send, "gy")

    pair = [(i, i ^ 1) for i in range(gz)]
    onward = [(i, i + 2) for i in range(0, gz - 2, 2)] + [(i, i - 2) for i in range(3, gz, 2)]
    near = [lax.ppermute(low, "gz", pair) for low in lows]
    far = [lax.ppermute(low, "gz", onward) for low in near]

    part, early = x_part(scal, drag_coef, jnp.asarray(fx), jnp.asarray(inv_x), lows, adj, wnd, classes)
    drift = swap(y_part(part, recv, jnp.asarray(line_tables(total_y))), "gy")
    rhs, adj, sums = join(scal, gate(early, far), part, wnd, classes, adj, near, far, drift, count)

    group, pairs = 2 * gy, gz // 2
    within = [[k * group + i for i in range(group)] for k in range(pairs)]
    across = [[k * group + i for k in range(pairs)] for i in range(group)]
    got = swap(fold(swap(sums, ("gz", "gy"), within), pairs, count), ("gz", "gy"), across)
    scale = 1.0 / math.sqrt(nx * total_y * gz / count)
    new, sens = finish(got, adj, rhs, count, scale)
    return new.reshape(adjoint.shape), sens.reshape(count)


def solution(mesh):
    return jax.shard_map(
        local,
        mesh=mesh,
        in_specs=(P(None, "gz", None, "gy"), P(None, "gz", None, "gy"), P(None, "gy"), P()),
        out_specs=(P(None, "gz", None, "gy"), P()),
        check_vma=False,
    )
```

```python
import functools
import math

import jax
import jax.numpy as jnp
import ml_dtypes
import numpy as np
from jax import lax
from jax.experimental import pallas as pl
from jax.experimental.pallas import tpu as pltpu
from jax.sharding import PartitionSpec as P

viscosity = 0.3
courant = 0.8
epsilon = 1e-06
LANES = 128
TILE = 256
VMEM_MIB = 16
f32 = jnp.float32
bf16 = jnp.bfloat16


@functools.lru_cache(maxsize=None)
def tables(length):
    half = length // 2
    modes = np.arange(half)
    points = np.arange(length)
    angles = (2.0 * np.pi / length) * ((modes[:, None] * points[None, :]) % length)
    cosine, sine = np.cos(angles), np.sin(angles)
    forward = np.concatenate([cosine, -sine], axis=0)
    wave = (2.0 * np.pi / length) * modes
    weight = np.where(modes == 0, 1.0, 2.0) / length
    w1, w2 = (weight * wave)[:, None], (weight * wave * wave)[:, None]
    first = np.concatenate([-w1 * sine, -w1 * cosine], axis=0).T
    second = np.concatenate([-w2 * cosine, w2 * sine], axis=0).T
    low = lambda a: np.ascontiguousarray(a).astype(ml_dtypes.bfloat16)
    return low(forward), low(first), low(second)


@functools.lru_cache(maxsize=None)
def line_tables(length):
    half = length // 2
    modes = np.arange(half)
    angles = (2.0 * np.pi / length) * ((modes[:, None] * np.arange(length)[None, :]) % length)
    wave = (2.0 * np.pi / length) * modes
    weight = np.where(modes == 0, 1.0, 2.0) / length
    first = -(weight * wave) @ np.sin(angles)
    second = -(weight * wave * wave) @ np.cos(angles)
    gap = np.arange(half)[None, :] - np.arange(half)[:, None]
    made = []
    for row in (first, second):
        a, b = row[gap % length], row[(gap + half) % length]
        made += [0.5 * (a + b), 0.5 * (a - b)]
    every = np.stack(made).reshape(4, half, half // TILE, TILE).transpose(2, 0, 1, 3)
    return np.ascontiguousarray(every).astype(ml_dtypes.bfloat16)


CHUNKS = 4
SUB = 64
GATE_FLOPS = 10**10


def params(mib=VMEM_MIB, **more):
    return pltpu.CompilerParams(vmem_limit_bytes=mib * 1024 * 1024, **more)


def begin(copies, sems, first=0):
    made = [pltpu.make_async_copy(src, dst, sems.at[first + n]) for n, (src, dst) in enumerate(copies)]
    for copy in made:
        copy.start()
    return made


def finish_all(made):
    for copy in made:
        copy.wait()


def full(shape):
    return pl.BlockSpec(shape, lambda i: (0,) * len(shape))


SMEM = pl.BlockSpec(memory_space=pltpu.SMEM)
HBM = pl.BlockSpec(memory_space=pltpu.HBM)
SMALL = pl.BlockSpec(memory_space=pltpu.VMEM)
near_by = functools.partial(pltpu.with_memory_space_constraint, memory_space=pltpu.VMEM)
far_off = functools.partial(pltpu.with_memory_space_constraint, memory_space=pltpu.HBM)


def dot(a, b):
    return jnp.dot(a, b, preferred_element_type=f32)


def pack_kernel(adj, wind, send, l0, l1, l2, adj_v, wind_v, send_v, lows_v, sem_in, sem_out):
    parts, _, rows, _ = send.shape
    per = parts // CHUNKS
    loads, stores = [], []
    for k in range(CHUNKS):
        at = pl.ds(k * per * rows, per * rows)
        loads.append(begin([(adj.at[:, at], adj_v.at[:, at]), (wind.at[1, at], wind_v.at[at])], sem_in, 2 * k))
    for k in range(CHUNKS):
        finish_all(loads[k])
        for s in range(k * per, (k + 1) * per):
            at = slice(s * rows, (s + 1) * rows)
            for c in range(3):
                low = adj_v[c, at].astype(bf16)
                send_v[s, c] = low
                lows_v[c, at] = low
            send_v[s, 3] = wind_v[at]
        at, part = pl.ds(k * per * rows, per * rows), pl.ds(k * per, per)
        stores += begin([(send_v.at[part], send.at[part])]
                        + [(lows_v.at[c, at], low.at[at]) for c, low in enumerate((l0, l1, l2))], sem_out, 4 * k)
    finish_all(stores)


def pack(adj, wind, parts):
    _, nx, ny = adj.shape
    rows = nx // parts
    sent, kept = (parts, 4, rows, ny), (3, nx, ny)
    return pl.pallas_call(
        pack_kernel,
        in_specs=[HBM, HBM],
        out_specs=[HBM] * 4,
        out_shape=[pltpu.HBM(sent, bf16)] + [pltpu.HBM((nx, ny), bf16)] * 3,
        scratch_shapes=[pltpu.VMEM(kept, f32), pltpu.VMEM((nx, ny), bf16), pltpu.VMEM(sent, bf16), pltpu.VMEM(kept, bf16),
                        pltpu.SemaphoreType.DMA((2 * CHUNKS,)), pltpu.SemaphoreType.DMA((4 * CHUNKS,))],
        compiler_params=params(),
        cost_estimate=pl.CostEstimate(flops=0, bytes_accessed=nx * ny * 32, transcendentals=0),
        name="pack",
    )(far_off(adj), far_off(wind))


def speed_of(w):
    return jnp.sqrt(w[0] * w[0] + w[1] * w[1] + w[2] * w[2])


def class_sums(column, cls, acc, count):
    for k in range(count):
        kept = jnp.where(cls == k, column, 0.0)
        acc[k] += jnp.sum(kept.reshape(-1, 8, kept.shape[-1]), axis=0)


def to_lanes(acc, count, offset):
    per = jnp.sum(acc[...], axis=1)
    per = jnp.sum(per, axis=1, keepdims=True)
    row = lax.broadcasted_iota(jnp.int32, (count, LANES), 0)
    lane = lax.broadcasted_iota(jnp.int32, (count, LANES), 1)
    return jnp.sum(jnp.where(lane == row + offset, per, 0.0), axis=0, keepdims=True)


def x_kernel(after, fwd, inv, l0, l1, l2, wind, rhs, low, spec, fwd_v, inv_v, wind_v, rhs_v, sem_l, sem_f, sem_i, sem_o):
    nx, ny = l0.shape
    steps = nx // TILE
    ats = [pl.ds(t * TILE, TILE) for t in range(steps)]
    lines = begin([(ref, low.at[:, pl.ds(c * ny, ny)]) for c, ref in enumerate((l0, l1, l2))], sem_l)
    tiles = begin([(fwd.at[at], fwd_v.at[at]) for at in ats], sem_f)
    loads = [begin([(inv.at[t], inv_v.at[t]), (wind.at[0, at], wind_v.at[at])], sem_i, 2 * t) for t, at in enumerate(ats)]
    finish_all(lines)
    for t in range(0, steps, 2):
        finish_all(tiles[t:t + 2])
        at = slice(t * TILE, (t + 2) * TILE)
        spec[at] = dot(fwd_v[at], low[...]).astype(bf16)
    stores = []
    for t, at in enumerate(ats):
        finish_all(loads[t])
        both = dot(inv_v[t], spec[...])
        for r in range(0, TILE, SUB):
            sub = slice(t * TILE + r, t * TILE + r + SUB)
            w0 = wind_v[sub].astype(f32)
            for c in range(3):
                cols = slice(c * ny, (c + 1) * ny)
                rhs_v[c, sub] = w0 * both[r:r + SUB, cols] + viscosity * both[TILE + r:TILE + r + SUB, cols]
        stores += begin([(rhs_v.at[:, at], rhs.at[:, at])], sem_o, t)
    finish_all(stores)


def x_part(after, fwd, inv, lows, wind):
    _, nx, ny = wind.shape
    steps = nx // TILE
    dma = pltpu.SemaphoreType.DMA
    return pl.pallas_call(
        x_kernel,
        in_specs=[SMEM] + [HBM] * 6,
        out_specs=HBM,
        out_shape=pltpu.HBM((3, nx, ny), f32),
        scratch_shapes=[pltpu.VMEM((nx, 3 * ny), bf16), pltpu.VMEM((nx, 3 * ny), bf16),
                        pltpu.VMEM(fwd.shape, bf16), pltpu.VMEM(inv.shape, bf16),
                        pltpu.VMEM((nx, ny), bf16), pltpu.VMEM((3, nx, ny), f32),
                        dma((3,)), dma((steps,)), dma((2 * steps,)), dma((steps,))],
        compiler_params=params(32),
        cost_estimate=pl.CostEstimate(flops=6 * nx * nx * 3 * ny, bytes_accessed=12 * 1024 * 1024, transcendentals=0),
        name="x_part",
    )(after, far_off(fwd), far_off(inv), *[far_off(low) for low in lows], far_off(wind))


def y_kernel(after, recv, table, out, plus, minus, table_v, out_v, sem_t, sem_o):
    parts, _, rows, ny = recv.shape
    half, steps = parts // 2, table.shape[0]
    tiles = begin([(table.at[t], table_v.at[t]) for t in range(steps)], sem_t)
    for s in range(half):
        for c in range(3):
            u, v = recv[s, c].astype(f32), recv[s + half, c].astype(f32)
            at = (slice(c * rows, (c + 1) * rows), slice(s * ny, (s + 1) * ny))
            plus[at] = (u + v).astype(bf16)
            minus[at] = (u - v).astype(bf16)
    per = TILE // ny
    stores = []
    for t in range(steps):
        tiles[t].wait()
        p1, q1 = dot(plus[...], table_v[t, 0]), dot(minus[...], table_v[t, 1])
        p2, q2 = dot(plus[...], table_v[t, 2]), dot(minus[...], table_v[t, 3])
        for s in range(per):
            cols = slice(s * ny, (s + 1) * ny)
            a, b = t * per + s, half + t * per + s
            for r in range(0, rows, SUB):
                sub = slice(r, r + SUB)
                wa, wb = recv[a, 3, sub].astype(f32), recv[b, 3, sub].astype(f32)
                for c in range(3):
                    at = slice(c * rows + r, c * rows + r + SUB)
                    u1, v1, u2, v2 = (m[at, cols] for m in (p1, q1, p2, q2))
                    out_v[a, c, sub] = (wa * (u1 + v1) + viscosity * (u2 + v2)).astype(bf16)
                    out_v[b, c, sub] = (wb * (u1 - v1) + viscosity * (u2 - v2)).astype(bf16)
        ends = [pl.ds(base, per) for base in (t * per, half + t * per)]
        stores += begin([(out_v.at[e], out.at[e]) for e in ends], sem_o, 2 * t)
    finish_all(stores)


def y_part(after, recv, table):
    parts, _, rows, ny = recv.shape
    n, steps = parts * ny, table.shape[0]
    sent = (parts, 3, rows, ny)
    dma = pltpu.SemaphoreType.DMA
    return pl.pallas_call(
        y_kernel,
        in_specs=[HBM, SMALL, HBM],
        out_specs=HBM,
        out_shape=pltpu.HBM(sent, bf16),
        scratch_shapes=[pltpu.VMEM((3 * rows, n // 2), bf16), pltpu.VMEM((3 * rows, n // 2), bf16),
                        pltpu.VMEM(table.shape, bf16), pltpu.VMEM(sent, bf16), dma((steps,)), dma((2 * steps,))],
        compiler_params=params(),
        cost_estimate=pl.CostEstimate(flops=2 * n * n * 3 * rows, bytes_accessed=4 * 1024 * 1024, transcendentals=0),
        name="y_part",
    )(far_off(after), near_by(recv), far_off(table))


def gate_kernel(early, q0, q1, q2, out):
    out[...] = early[...]


def gate(early, far):
    return pl.pallas_call(
        gate_kernel,
        in_specs=[SMALL, HBM, HBM, SMALL],
        out_specs=SMALL,
        out_shape=jax.ShapeDtypeStruct(early.shape, f32),
        compiler_params=params(4),
        cost_estimate=pl.CostEstimate(flops=GATE_FLOPS, bytes_accessed=1024, transcendentals=0),
        name="gate",
    )(early, *[far_off(q) for q in far[:2]], near_by(far[2]))


def local_kernel(count, scal, coef, part, wind, classes, adj, p0, p1, p2, q0, rhs, sums,
                 part_v, wind_v, cls_v, adj_v, near_v, far_v, first, second, top, sem_in, sem_out):
    nx, ny = classes.shape
    rows = nx // CHUNKS
    loads, stores = [], []
    for k in range(CHUNKS):
        at = pl.ds(k * rows, rows)
        loads.append(begin([(a.at[:, at], b.at[:, at]) for a, b in ((wind, wind_v), (part, part_v), (adj, adj_v))]
                           + [(classes.at[at], cls_v.at[at]), (q0.at[at], far_v.at[at])]
                           + [(p.at[at], near_v.at[c, at]) for c, p in enumerate((p0, p1, p2))], sem_in, 8 * k))
    for ref in (first, second, top):
        ref[...] = jnp.zeros_like(ref)
    for k in range(CHUNKS):
        finish_all(loads[k])
        for n in range(k * rows // SUB, (k + 1) * rows // SUB):
            at = slice(n * SUB, (n + 1) * SUB)
            cls = cls_v[at]
            w = [wind_v[c, at].astype(f32) for c in range(3)]
            size = jnp.abs(w[0]) + jnp.abs(w[1]) + jnp.abs(w[2])
            top[...] = jnp.maximum(top[...], jnp.max(size.reshape(-1, 8, ny), axis=0))
            weight = scal[0] * speed_of(w)
            drag = jnp.zeros_like(weight)
            for m in range(count):
                drag = jnp.where(cls == m, coef[m], drag)
            damp = drag * weight + 2.0 * viscosity
            slope = (0.5 * scal[1]) * w[2]
            held, moved = jnp.zeros_like(weight), jnp.zeros_like(weight)
            for c in range(3):
                a = adj_v[c, at]
                r = part_v[c, at] - damp * a + (viscosity + slope) * near_v[c, at].astype(f32)
                if c == 0:
                    r += (viscosity - slope) * far_v[at].astype(f32)
                part_v[c, at] = r
                held += a * w[c]
                moved += r * w[c]
            class_sums(weight * held, cls, first, count)
            class_sums(weight * moved, cls, second, count)
        at = pl.ds(k * rows, rows)
        stores += begin([(part_v.at[:, at], rhs.at[:, at])], sem_out, k)
    lane = lax.broadcasted_iota(jnp.int32, (1, LANES), 1)
    peak = jnp.max(jnp.max(top[...], axis=0, keepdims=True), axis=1, keepdims=True)
    both = to_lanes(first, count, 0) + to_lanes(second, count, count)
    sums[...] = jnp.where(lane == 2 * count, peak, both)
    finish_all(stores)


def local_part(scal, coef, part, wind, classes, adj, near, far):
    _, nx, ny = part.shape
    count = coef.shape[0]
    whole = (3, nx, ny)
    dma = pltpu.SemaphoreType.DMA
    return pl.pallas_call(
        functools.partial(local_kernel, count),
        in_specs=[SMEM, SMEM] + [HBM] * 8,
        out_specs=[HBM, SMALL],
        out_shape=[pltpu.HBM(whole, f32), jax.ShapeDtypeStruct((1, LANES), f32)],
        scratch_shapes=[pltpu.VMEM(whole, f32), pltpu.VMEM(whole, bf16), pltpu.VMEM((nx, ny), jnp.int32),
                        pltpu.VMEM(whole, f32), pltpu.VMEM(whole, bf16), pltpu.VMEM((nx, ny), bf16),
                        pltpu.VMEM((count, 8, ny), f32), pltpu.VMEM((count, 8, ny), f32), pltpu.VMEM((8, ny), f32),
                        dma((8 * CHUNKS,)), dma((CHUNKS,))],
        compiler_params=params(),
        cost_estimate=pl.CostEstimate(flops=200 * nx * ny, bytes_accessed=8 * 1024 * 1024, transcendentals=0),
        name="local_part",
    )(scal, coef, *[far_off(a) for a in (part, wind, classes, adj, *near, far)])


def join_kernel(count, scal, early, part, wind, classes, adj, q1, q2, drift, rhs, adj_v, sums,
                wind_v, cls_v, far_v, acc, sem_in, sem_adj):
    parts, _, rows, _ = drift.shape
    per = parts // CHUNKS
    loads = []
    for k in range(CHUNKS):
        at = pl.ds(k * per * rows, per * rows)
        loads.append(begin([(wind.at[:, at], wind_v.at[:, at]), (classes.at[at], cls_v.at[at]),
                            (part.at[:, at], rhs.at[:, at]), (q1.at[at], far_v.at[at])], sem_in, 4 * k))
    kept = begin([(adj, adj_v)], sem_adj)
    acc[...] = jnp.zeros_like(acc)
    for k in range(CHUNKS):
        finish_all(loads[k])
        for n in range(k * per * rows // SUB, (k + 1) * per * rows // SUB):
            at = slice(n * SUB, (n + 1) * SUB)
            s, sub = n * SUB // rows, slice(n * SUB % rows, n * SUB % rows + SUB)
            w = [wind_v[c, at].astype(f32) for c in range(3)]
            down = viscosity - (0.5 * scal[1]) * w[2]
            total = jnp.zeros_like(down)
            for c in range(3):
                r = drift[s, c, sub].astype(f32)
                if c > 0:
                    r += down * (far_v[at] if c == 1 else q2[at]).astype(f32)
                rhs[c, at] = rhs[c, at] + r
                total += r * w[c]
            class_sums(scal[0] * speed_of(w) * total, cls_v[at], acc, count)
    sums[...] = jnp.broadcast_to((early[...] + to_lanes(acc, count, count))[None], sums.shape)
    finish_all(kept)


def join(scal, early, part, wind, classes, adj, far, drift, count):
    parts, _, rows, ny = drift.shape
    nx = parts * rows
    whole = (3, nx, ny)
    dma = pltpu.SemaphoreType.DMA
    return pl.pallas_call(
        functools.partial(join_kernel, count),
        in_specs=[SMEM, SMALL] + [HBM] * 5 + [SMALL] * 2,
        out_specs=[SMALL, SMALL, SMALL],
        out_shape=[pltpu.VMEM(whole, f32), pltpu.VMEM(whole, f32), jax.ShapeDtypeStruct((2 * parts, 1, LANES), f32)],
        scratch_shapes=[pltpu.VMEM(whole, bf16), pltpu.VMEM((nx, ny), jnp.int32), pltpu.VMEM((nx, ny), bf16),
                        pltpu.VMEM((count, 8, ny), f32), dma((4 * CHUNKS,)), dma((1,))],
        compiler_params=params(),
        cost_estimate=pl.CostEstimate(flops=100 * nx * ny, bytes_accessed=8 * 1024 * 1024, transcendentals=0),
        name="join",
    )(scal, early, *[far_off(a) for a in (part, wind, classes, adj, far[0])], near_by(far[1]), near_by(drift))


def merge(rows, count):
    lane = lax.broadcasted_iota(jnp.int32, (1, LANES), 1)
    return jnp.where(lane == 2 * count, jnp.max(rows, axis=0), jnp.sum(rows, axis=0))


def fold_kernel(count, got, out):
    out[...] = jnp.broadcast_to(merge(got[...], count)[None], out.shape)


def fold(got, size, count):
    return pl.pallas_call(
        functools.partial(fold_kernel, count),
        out_shape=jax.ShapeDtypeStruct((size, 1, LANES), f32),
        compiler_params=params(4),
        name="fold",
    )(got)


def finish_kernel(count, scale, got, adj, rhs, new, sens, new_v, sems):
    nx = adj.shape[1]
    rows = nx // CHUNKS
    sums = merge(got[...], count)
    lane = lax.broadcasted_iota(jnp.int32, (1, LANES), 1)
    top = jnp.max(jnp.where(lane == 2 * count, sums, 0.0), axis=1, keepdims=True)
    step = courant / (top + epsilon)
    stores = []
    for k in range(CHUNKS):
        at = slice(k * rows, (k + 1) * rows)
        for c in range(3):
            new_v[c, at] = adj[c, at] + step * rhs[c, at]
        at = pl.ds(k * rows, rows)
        stores += begin([(new_v.at[:, at], new.at[:, at])], sems, k)
    later = pltpu.roll(sums, LANES - count, 1)
    sens[...] = (-step * scale * (sums + step * later))[:, :count]
    finish_all(stores)


def finish(got, adj, rhs, count, scale):
    return pl.pallas_call(
        functools.partial(finish_kernel, count, scale),
        in_specs=[SMALL, SMALL, SMALL],
        out_specs=[HBM, SMALL],
        out_shape=[pltpu.HBM(adj.shape, f32), jax.ShapeDtypeStruct((1, count), f32)],
        scratch_shapes=[pltpu.VMEM(adj.shape, f32), pltpu.SemaphoreType.DMA((CHUNKS,))],
        compiler_params=params(),
        cost_estimate=pl.CostEstimate(flops=2 * adj.size, bytes_accessed=12 * adj.size, transcendentals=0),
        name="finish",
    )(got, near_by(adj), near_by(rhs))


def swap(x, axes, groups=None):
    return lax.all_to_all(x, axes, split_axis=0, concat_axis=0, axis_index_groups=groups, tiled=True)


def local(adjoint, wind, classes, drag_coef):
    gz, gy = lax.axis_size("gz"), lax.axis_size("gy")
    _, _, nx, ny = adjoint.shape
    total_y = ny * gy
    count = drag_coef.shape[0]
    adj = adjoint.reshape(3, nx, ny)
    wnd = wind.reshape(3, nx, ny)

    fx, d1x, d2x = tables(nx)
    inv_x = np.concatenate([d1x.reshape(-1, TILE, nx), d2x.reshape(-1, TILE, nx)], axis=1)

    me = lax.axis_index("gz")
    height = jnp.exp(-2.0 * (me.astype(f32) + 0.5) / gz)
    sign = jnp.where(me % 2 == 0, 1.0, -1.0).astype(f32)
    scal = jnp.stack([height, sign])

    send, *lows = pack(adj, wnd, gy)
    recv = swap(send, "gy")

    pair = [(i, i ^ 1) for i in range(gz)]
    onward = [(i, i + 2) for i in range(0, gz - 2, 2)] + [(i, i - 2) for i in range(3, gz, 2)]
    near = [lax.ppermute(low, "gz", pair) for low in lows]
    far = [lax.ppermute(low, "gz", onward) for low in near]

    part = x_part(scal, jnp.asarray(fx), jnp.asarray(inv_x), lows, wnd)
    drift = swap(y_part(part, recv, jnp.asarray(line_tables(total_y))), "gy")
    part, early = local_part(scal, drag_coef, part, wnd, classes, adj, near, far[0])
    rhs, adj, sums = join(scal, gate(early, far), part, wnd, classes, adj, far[1:], drift, count)

    group, pairs = 2 * gy, gz // 2
    within = [[k * group + i for i in range(group)] for k in range(pairs)]
    across = [[k * group + i for k in range(pairs)] for i in range(group)]
    got = swap(fold(swap(sums, ("gz", "gy"), within), pairs, count), ("gz", "gy"), across)
    scale = 1.0 / math.sqrt(nx * total_y * gz / count)
    new, sens = finish(got, adj, rhs, count, scale)
    return new.reshape(adjoint.shape), sens.reshape(count)


def solution(mesh):
    return jax.shard_map(
        local,
        mesh=mesh,
        in_specs=(P(None, "gz", None, "gy"), P(None, "gz", None, "gy"), P(None, "gy"), P()),
        out_specs=(P(None, "gz", None, "gy"), P()),
        check_vma=False,
    )
```

```python
import functools
import math

import jax
import jax.numpy as jnp
import ml_dtypes
import numpy as np
from jax import lax
from jax.experimental import pallas as pl
from jax.experimental.pallas import tpu as pltpu
from jax.sharding import PartitionSpec as P

viscosity = 0.3
courant = 0.8
epsilon = 1e-06
LANES = 128
TILE = 256
VMEM_MIB = 16
f32 = jnp.float32
bf16 = jnp.bfloat16


@functools.lru_cache(maxsize=None)
def tables(length):
    half = length // 2
    modes = np.arange(half)
    points = np.arange(length)
    angles = (2.0 * np.pi / length) * ((modes[:, None] * points[None, :]) % length)
    cosine, sine = np.cos(angles), np.sin(angles)
    forward = np.concatenate([cosine, -sine], axis=0)
    wave = (2.0 * np.pi / length) * modes
    weight = np.where(modes == 0, 1.0, 2.0) / length
    w1, w2 = (weight * wave)[:, None], (weight * wave * wave)[:, None]
    first = np.concatenate([-w1 * sine, -w1 * cosine], axis=0).T
    second = np.concatenate([-w2 * cosine, w2 * sine], axis=0).T
    low = lambda a: np.ascontiguousarray(a).astype(ml_dtypes.bfloat16)
    return low(forward), low(first), low(second)


@functools.lru_cache(maxsize=None)
def line_tables(length):
    half = length // 2
    modes = np.arange(half)
    angles = (2.0 * np.pi / length) * ((modes[:, None] * np.arange(length)[None, :]) % length)
    wave = (2.0 * np.pi / length) * modes
    weight = np.where(modes == 0, 1.0, 2.0) / length
    first = -(weight * wave) @ np.sin(angles)
    second = -(weight * wave * wave) @ np.cos(angles)
    gap = np.arange(half)[None, :] - np.arange(half)[:, None]
    made = []
    for row in (first, second):
        a, b = row[gap % length], row[(gap + half) % length]
        made += [0.5 * (a + b), 0.5 * (a - b)]
    every = np.stack(made).reshape(4, half, half // TILE, TILE).transpose(2, 0, 1, 3)
    return np.ascontiguousarray(every).astype(ml_dtypes.bfloat16)


CHUNKS = 4
SUB = 64
GATE_FLOPS = 10**10


def params(mib=VMEM_MIB, **more):
    return pltpu.CompilerParams(vmem_limit_bytes=mib * 1024 * 1024, **more)


def begin(copies, sems, first=0):
    made = [pltpu.make_async_copy(src, dst, sems.at[first + n]) for n, (src, dst) in enumerate(copies)]
    for copy in made:
        copy.start()
    return made


def finish_all(made):
    for copy in made:
        copy.wait()


def full(shape):
    return pl.BlockSpec(shape, lambda i: (0,) * len(shape))


SMEM = pl.BlockSpec(memory_space=pltpu.SMEM)
HBM = pl.BlockSpec(memory_space=pltpu.HBM)
SMALL = pl.BlockSpec(memory_space=pltpu.VMEM)
near_by = functools.partial(pltpu.with_memory_space_constraint, memory_space=pltpu.VMEM)
far_off = functools.partial(pltpu.with_memory_space_constraint, memory_space=pltpu.HBM)


def dot(a, b):
    return jnp.dot(a, b, preferred_element_type=f32)


def pack_kernel(adj, wind, send, l0, l1, l2, adj_v, wind_v, send_v, lows_v, sem_in, sem_out):
    parts, _, rows, _ = send.shape
    per = parts // CHUNKS
    loads, stores = [], []
    for k in range(CHUNKS):
        at = pl.ds(k * per * rows, per * rows)
        loads.append(begin([(adj.at[:, at], adj_v.at[:, at]), (wind.at[1, at], wind_v.at[at])], sem_in, 2 * k))
    for k in range(CHUNKS):
        finish_all(loads[k])
        for s in range(k * per, (k + 1) * per):
            at = slice(s * rows, (s + 1) * rows)
            for c in range(3):
                low = adj_v[c, at].astype(bf16)
                send_v[s, c] = low
                lows_v[c, at] = low
            send_v[s, 3] = wind_v[at]
        at, part = pl.ds(k * per * rows, per * rows), pl.ds(k * per, per)
        stores += begin([(send_v.at[part], send.at[part])]
                        + [(lows_v.at[c, at], low.at[at]) for c, low in enumerate((l0, l1, l2))], sem_out, 4 * k)
    finish_all(stores)


def pack(adj, wind, parts):
    _, nx, ny = adj.shape
    rows = nx // parts
    sent, kept = (parts, 4, rows, ny), (3, nx, ny)
    return pl.pallas_call(
        pack_kernel,
        in_specs=[HBM, HBM],
        out_specs=[HBM] * 4,
        out_shape=[pltpu.HBM(sent, bf16)] + [pltpu.HBM((nx, ny), bf16)] * 3,
        scratch_shapes=[pltpu.VMEM(kept, f32), pltpu.VMEM((nx, ny), bf16), pltpu.VMEM(sent, bf16), pltpu.VMEM(kept, bf16),
                        pltpu.SemaphoreType.DMA((2 * CHUNKS,)), pltpu.SemaphoreType.DMA((4 * CHUNKS,))],
        compiler_params=params(),
        cost_estimate=pl.CostEstimate(flops=0, bytes_accessed=nx * ny * 32, transcendentals=0),
        name="pack",
    )(far_off(adj), far_off(wind))


def speed_of(w):
    return jnp.sqrt(w[0] * w[0] + w[1] * w[1] + w[2] * w[2])


def class_sums(column, cls, acc, count):
    for k in range(count):
        kept = jnp.where(cls == k, column, 0.0)
        acc[k] += jnp.sum(kept.reshape(-1, 8, kept.shape[-1]), axis=0)


def to_lanes(acc, count, offset):
    per = jnp.sum(acc[...], axis=1)
    per = jnp.sum(per, axis=1, keepdims=True)
    row = lax.broadcasted_iota(jnp.int32, (count, LANES), 0)
    lane = lax.broadcasted_iota(jnp.int32, (count, LANES), 1)
    return jnp.sum(jnp.where(lane == row + offset, per, 0.0), axis=0, keepdims=True)


def x_kernel(after, fwd, inv, l0, l1, l2, wind, rhs, low, spec, fwd_v, inv_v, wind_v, rhs_v, sem_l, sem_f, sem_i, sem_o):
    nx, ny = l0.shape
    steps = nx // TILE
    ats = [pl.ds(t * TILE, TILE) for t in range(steps)]
    lines = begin([(ref, low.at[:, pl.ds(c * ny, ny)]) for c, ref in enumerate((l0, l1, l2))], sem_l)
    tiles = begin([(fwd.at[at], fwd_v.at[at]) for at in ats], sem_f)
    loads = [begin([(inv.at[t], inv_v.at[t]), (wind.at[0, at], wind_v.at[at])], sem_i, 2 * t) for t, at in enumerate(ats)]
    finish_all(lines)
    for t in range(0, steps, 2):
        finish_all(tiles[t:t + 2])
        at = slice(t * TILE, (t + 2) * TILE)
        spec[at] = dot(fwd_v[at], low[...]).astype(bf16)
    stores = []
    for t, at in enumerate(ats):
        finish_all(loads[t])
        both = dot(inv_v[t], spec[...])
        for r in range(0, TILE, SUB):
            sub = slice(t * TILE + r, t * TILE + r + SUB)
            w0 = wind_v[sub].astype(f32)
            for c in range(3):
                cols = slice(c * ny, (c + 1) * ny)
                rhs_v[c, sub] = w0 * both[r:r + SUB, cols] + viscosity * both[TILE + r:TILE + r + SUB, cols]
        stores += begin([(rhs_v.at[:, at], rhs.at[:, at])], sem_o, t)
    finish_all(stores)


def x_part(after, fwd, inv, lows, wind):
    _, nx, ny = wind.shape
    steps = nx // TILE
    dma = pltpu.SemaphoreType.DMA
    return pl.pallas_call(
        x_kernel,
        in_specs=[SMEM] + [HBM] * 6,
        out_specs=HBM,
        out_shape=pltpu.HBM((3, nx, ny), f32),
        scratch_shapes=[pltpu.VMEM((nx, 3 * ny), bf16), pltpu.VMEM((nx, 3 * ny), bf16),
                        pltpu.VMEM(fwd.shape, bf16), pltpu.VMEM(inv.shape, bf16),
                        pltpu.VMEM((nx, ny), bf16), pltpu.VMEM((3, nx, ny), f32),
                        dma((3,)), dma((steps,)), dma((2 * steps,)), dma((steps,))],
        compiler_params=params(32),
        cost_estimate=pl.CostEstimate(flops=6 * nx * nx * 3 * ny, bytes_accessed=12 * 1024 * 1024, transcendentals=0),
        name="x_part",
    )(after, far_off(fwd), far_off(inv), *[far_off(low) for low in lows], far_off(wind))


def y_kernel(after, recv, table_v, out, plus, minus, out_v, sem_o):
    parts, _, rows, ny = recv.shape
    half, steps = parts // 2, table_v.shape[0]
    for s in range(half):
        for c in range(3):
            u, v = recv[s, c].astype(f32), recv[s + half, c].astype(f32)
            at = (slice(c * rows, (c + 1) * rows), slice(s * ny, (s + 1) * ny))
            plus[at] = (u + v).astype(bf16)
            minus[at] = (u - v).astype(bf16)
    per = TILE // ny
    stores = []
    for t in range(steps):
        p1, q1 = dot(plus[...], table_v[t, 0]), dot(minus[...], table_v[t, 1])
        p2, q2 = dot(plus[...], table_v[t, 2]), dot(minus[...], table_v[t, 3])
        for s in range(per):
            cols = slice(s * ny, (s + 1) * ny)
            a, b = t * per + s, half + t * per + s
            for r in range(0, rows, SUB):
                sub = slice(r, r + SUB)
                wa, wb = recv[a, 3, sub].astype(f32), recv[b, 3, sub].astype(f32)
                for c in range(3):
                    at = slice(c * rows + r, c * rows + r + SUB)
                    u1, v1, u2, v2 = (m[at, cols] for m in (p1, q1, p2, q2))
                    out_v[a, c, sub] = (wa * (u1 + v1) + viscosity * (u2 + v2)).astype(bf16)
                    out_v[b, c, sub] = (wb * (u1 - v1) + viscosity * (u2 - v2)).astype(bf16)
        ends = [pl.ds(base, per) for base in (t * per, half + t * per)]
        stores += begin([(out_v.at[e], out.at[e]) for e in ends], sem_o, 2 * t)
    finish_all(stores)


def y_part(after, recv, table):
    parts, _, rows, ny = recv.shape
    n, steps = parts * ny, table.shape[0]
    sent = (parts, 3, rows, ny)
    dma = pltpu.SemaphoreType.DMA
    return pl.pallas_call(
        y_kernel,
        in_specs=[HBM, SMALL, SMALL],
        out_specs=HBM,
        out_shape=pltpu.HBM(sent, bf16),
        scratch_shapes=[pltpu.VMEM((3 * rows, n // 2), bf16), pltpu.VMEM((3 * rows, n // 2), bf16),
                        pltpu.VMEM(sent, bf16), dma((2 * steps,))],
        compiler_params=params(),
        cost_estimate=pl.CostEstimate(flops=2 * n * n * 3 * rows, bytes_accessed=4 * 1024 * 1024, transcendentals=0),
        name="y_part",
    )(far_off(after), near_by(recv), near_by(table))


def gate_kernel(early, q0, q1, q2, out):
    out[...] = early[...]


def gate(early, far):
    return pl.pallas_call(
        gate_kernel,
        in_specs=[SMALL, HBM, HBM, SMALL],
        out_specs=SMALL,
        out_shape=jax.ShapeDtypeStruct(early.shape, f32),
        compiler_params=params(4),
        cost_estimate=pl.CostEstimate(flops=GATE_FLOPS, bytes_accessed=1024, transcendentals=0),
        name="gate",
    )(early, *[far_off(q) for q in far[:2]], near_by(far[2]))


def local_kernel(count, scal, coef, part, wind, classes, adj, p0, p1, p2, q0, rhs, sums,
                 part_v, wind_v, cls_v, adj_v, near_v, far_v, first, second, top, sem_in, sem_out):
    nx, ny = classes.shape
    rows = nx // CHUNKS
    loads, stores = [], []
    for k in range(CHUNKS):
        at = pl.ds(k * rows, rows)
        loads.append(begin([(a.at[:, at], b.at[:, at]) for a, b in ((wind, wind_v), (part, part_v), (adj, adj_v))]
                           + [(classes.at[at], cls_v.at[at]), (q0.at[at], far_v.at[at])]
                           + [(p.at[at], near_v.at[c, at]) for c, p in enumerate((p0, p1, p2))], sem_in, 8 * k))
    for ref in (first, second, top):
        ref[...] = jnp.zeros_like(ref)
    for k in range(CHUNKS):
        finish_all(loads[k])
        for n in range(k * rows // SUB, (k + 1) * rows // SUB):
            at = slice(n * SUB, (n + 1) * SUB)
            cls = cls_v[at]
            w = [wind_v[c, at].astype(f32) for c in range(3)]
            size = jnp.abs(w[0]) + jnp.abs(w[1]) + jnp.abs(w[2])
            top[...] = jnp.maximum(top[...], jnp.max(size.reshape(-1, 8, ny), axis=0))
            weight = scal[0] * speed_of(w)
            drag = jnp.zeros_like(weight)
            for m in range(count):
                drag = jnp.where(cls == m, coef[m], drag)
            damp = drag * weight + 2.0 * viscosity
            slope = (0.5 * scal[1]) * w[2]
            held, moved = jnp.zeros_like(weight), jnp.zeros_like(weight)
            for c in range(3):
                a = adj_v[c, at]
                r = part_v[c, at] - damp * a + (viscosity + slope) * near_v[c, at].astype(f32)
                if c == 0:
                    r += (viscosity - slope) * far_v[at].astype(f32)
                part_v[c, at] = r
                held += a * w[c]
                moved += r * w[c]
            class_sums(weight * held, cls, first, count)
            class_sums(weight * moved, cls, second, count)
        at = pl.ds(k * rows, rows)
        stores += begin([(part_v.at[:, at], rhs.at[:, at])], sem_out, k)
    lane = lax.broadcasted_iota(jnp.int32, (1, LANES), 1)
    peak = jnp.max(jnp.max(top[...], axis=0, keepdims=True), axis=1, keepdims=True)
    both = to_lanes(first, count, 0) + to_lanes(second, count, count)
    sums[...] = jnp.where(lane == 2 * count, peak, both)
    finish_all(stores)


def local_part(scal, coef, part, wind, classes, adj, near, far):
    _, nx, ny = part.shape
    count = coef.shape[0]
    whole = (3, nx, ny)
    dma = pltpu.SemaphoreType.DMA
    return pl.pallas_call(
        functools.partial(local_kernel, count),
        in_specs=[SMEM, SMEM] + [HBM] * 8,
        out_specs=[HBM, SMALL],
        out_shape=[pltpu.HBM(whole, f32), jax.ShapeDtypeStruct((1, LANES), f32)],
        scratch_shapes=[pltpu.VMEM(whole, f32), pltpu.VMEM(whole, bf16), pltpu.VMEM((nx, ny), jnp.int32),
                        pltpu.VMEM(whole, f32), pltpu.VMEM(whole, bf16), pltpu.VMEM((nx, ny), bf16),
                        pltpu.VMEM((count, 8, ny), f32), pltpu.VMEM((count, 8, ny), f32), pltpu.VMEM((8, ny), f32),
                        dma((8 * CHUNKS,)), dma((CHUNKS,))],
        compiler_params=params(),
        cost_estimate=pl.CostEstimate(flops=200 * nx * ny, bytes_accessed=8 * 1024 * 1024, transcendentals=0),
        name="local_part",
    )(scal, coef, *[far_off(a) for a in (part, wind, classes, adj, *near, far)])


def join_kernel(count, scal, early, part, wind, classes, adj, q1, q2, drift, rhs, adj_v, sums,
                wind_v, cls_v, far_v, acc, sem_in, sem_adj):
    parts, _, rows, _ = drift.shape
    per = parts // CHUNKS
    loads = []
    for k in range(CHUNKS):
        at = pl.ds(k * per * rows, per * rows)
        loads.append(begin([(wind.at[:, at], wind_v.at[:, at]), (classes.at[at], cls_v.at[at]),
                            (part.at[:, at], rhs.at[:, at]), (q1.at[at], far_v.at[at])], sem_in, 4 * k))
    kept = begin([(adj, adj_v)], sem_adj)
    acc[...] = jnp.zeros_like(acc)
    for k in range(CHUNKS):
        finish_all(loads[k])
        for n in range(k * per * rows // SUB, (k + 1) * per * rows // SUB):
            at = slice(n * SUB, (n + 1) * SUB)
            s, sub = n * SUB // rows, slice(n * SUB % rows, n * SUB % rows + SUB)
            w = [wind_v[c, at].astype(f32) for c in range(3)]
            down = viscosity - (0.5 * scal[1]) * w[2]
            total = jnp.zeros_like(down)
            for c in range(3):
                r = drift[s, c, sub].astype(f32)
                if c > 0:
                    r += down * (far_v[at] if c == 1 else q2[at]).astype(f32)
                rhs[c, at] = rhs[c, at] + r
                total += r * w[c]
            class_sums(scal[0] * speed_of(w) * total, cls_v[at], acc, count)
    sums[...] = jnp.broadcast_to((early[...] + to_lanes(acc, count, count))[None], sums.shape)
    finish_all(kept)


def join(scal, early, part, wind, classes, adj, far, drift, count):
    parts, _, rows, ny = drift.shape
    nx = parts * rows
    whole = (3, nx, ny)
    dma = pltpu.SemaphoreType.DMA
    return pl.pallas_call(
        functools.partial(join_kernel, count),
        in_specs=[SMEM, SMALL] + [HBM] * 5 + [SMALL] * 2,
        out_specs=[SMALL, SMALL, SMALL],
        out_shape=[pltpu.VMEM(whole, f32), pltpu.VMEM(whole, f32), jax.ShapeDtypeStruct((2 * parts, 1, LANES), f32)],
        scratch_shapes=[pltpu.VMEM(whole, bf16), pltpu.VMEM((nx, ny), jnp.int32), pltpu.VMEM((nx, ny), bf16),
                        pltpu.VMEM((count, 8, ny), f32), dma((4 * CHUNKS,)), dma((1,))],
        compiler_params=params(),
        cost_estimate=pl.CostEstimate(flops=100 * nx * ny, bytes_accessed=8 * 1024 * 1024, transcendentals=0),
        name="join",
    )(scal, early, *[far_off(a) for a in (part, wind, classes, adj, far[0])], near_by(far[1]), near_by(drift))


def merge(rows, count):
    lane = lax.broadcasted_iota(jnp.int32, (1, LANES), 1)
    return jnp.where(lane == 2 * count, jnp.max(rows, axis=0), jnp.sum(rows, axis=0))


def fold_kernel(count, got, out):
    out[...] = jnp.broadcast_to(merge(got[...], count)[None], out.shape)


def fold(got, size, count):
    return pl.pallas_call(
        functools.partial(fold_kernel, count),
        out_shape=jax.ShapeDtypeStruct((size, 1, LANES), f32),
        compiler_params=params(4),
        name="fold",
    )(got)


def finish_kernel(count, scale, got, adj, rhs, new, sens, new_v, sems):
    nx = adj.shape[1]
    rows = nx // CHUNKS
    sums = merge(got[...], count)
    lane = lax.broadcasted_iota(jnp.int32, (1, LANES), 1)
    top = jnp.max(jnp.where(lane == 2 * count, sums, 0.0), axis=1, keepdims=True)
    step = courant / (top + epsilon)
    stores = []
    for k in range(CHUNKS):
        at = slice(k * rows, (k + 1) * rows)
        for c in range(3):
            new_v[c, at] = adj[c, at] + step * rhs[c, at]
        at = pl.ds(k * rows, rows)
        stores += begin([(new_v.at[:, at], new.at[:, at])], sems, k)
    later = pltpu.roll(sums, LANES - count, 1)
    sens[...] = (-step * scale * (sums + step * later))[:, :count]
    finish_all(stores)


def finish(got, adj, rhs, count, scale):
    return pl.pallas_call(
        functools.partial(finish_kernel, count, scale),
        in_specs=[SMALL, SMALL, SMALL],
        out_specs=[HBM, SMALL],
        out_shape=[pltpu.HBM(adj.shape, f32), jax.ShapeDtypeStruct((1, count), f32)],
        scratch_shapes=[pltpu.VMEM(adj.shape, f32), pltpu.SemaphoreType.DMA((CHUNKS,))],
        compiler_params=params(),
        cost_estimate=pl.CostEstimate(flops=2 * adj.size, bytes_accessed=12 * adj.size, transcendentals=0),
        name="finish",
    )(got, near_by(adj), near_by(rhs))


def swap(x, axes, groups=None):
    return lax.all_to_all(x, axes, split_axis=0, concat_axis=0, axis_index_groups=groups, tiled=True)


def local(adjoint, wind, classes, drag_coef):
    gz, gy = lax.axis_size("gz"), lax.axis_size("gy")
    _, _, nx, ny = adjoint.shape
    total_y = ny * gy
    count = drag_coef.shape[0]
    adj = adjoint.reshape(3, nx, ny)
    wnd = wind.reshape(3, nx, ny)

    fx, d1x, d2x = tables(nx)
    inv_x = np.concatenate([d1x.reshape(-1, TILE, nx), d2x.reshape(-1, TILE, nx)], axis=1)

    me = lax.axis_index("gz")
    height = jnp.exp(-2.0 * (me.astype(f32) + 0.5) / gz)
    sign = jnp.where(me % 2 == 0, 1.0, -1.0).astype(f32)
    scal = jnp.stack([height, sign])

    send, *lows = pack(adj, wnd, gy)
    recv = swap(send, "gy")

    pair = [(i, i ^ 1) for i in range(gz)]
    onward = [(i, i + 2) for i in range(0, gz - 2, 2)] + [(i, i - 2) for i in range(3, gz, 2)]
    near = [lax.ppermute(low, "gz", pair) for low in lows]
    far = [lax.ppermute(low, "gz", onward) for low in near]

    part = x_part(scal, jnp.asarray(fx), jnp.asarray(inv_x), lows, wnd)
    drift = swap(y_part(part, recv, jnp.asarray(line_tables(total_y))), "gy")
    part, early = local_part(scal, drag_coef, part, wnd, classes, adj, near, far[0])
    rhs, adj, sums = join(scal, gate(early, far), part, wnd, classes, adj, far[1:], drift, count)

    group, pairs = 2 * gy, gz // 2
    within = [[k * group + i for i in range(group)] for k in range(pairs)]
    across = [[k * group + i for k in range(pairs)] for i in range(group)]
    got = swap(fold(swap(sums, ("gz", "gy"), within), pairs, count), ("gz", "gy"), across)
    scale = 1.0 / math.sqrt(nx * total_y * gz / count)
    new, sens = finish(got, adj, rhs, count, scale)
    return new.reshape(adjoint.shape), sens.reshape(count)


def solution(mesh):
    return jax.shard_map(
        local,
        mesh=mesh,
        in_specs=(P(None, "gz", None, "gy"), P(None, "gz", None, "gy"), P(None, "gy"), P()),
        out_specs=(P(None, "gz", None, "gy"), P()),
        check_vma=False,
    )
```

```python
import functools
import math

import jax
import jax.numpy as jnp
import ml_dtypes
import numpy as np
from jax import lax
from jax.experimental import pallas as pl
from jax.experimental.pallas import tpu as pltpu
from jax.sharding import PartitionSpec as P

viscosity = 0.3
courant = 0.8
epsilon = 1e-06
LANES = 128
TILE = 256
VMEM_MIB = 16
f32 = jnp.float32
bf16 = jnp.bfloat16


@functools.lru_cache(maxsize=None)
def tables(length):
    half = length // 2
    modes = np.arange(half)
    points = np.arange(length)
    angles = (2.0 * np.pi / length) * ((modes[:, None] * points[None, :]) % length)
    cosine, sine = np.cos(angles), np.sin(angles)
    forward = np.concatenate([cosine, -sine], axis=0)
    wave = (2.0 * np.pi / length) * modes
    weight = np.where(modes == 0, 1.0, 2.0) / length
    w1, w2 = (weight * wave)[:, None], (weight * wave * wave)[:, None]
    first = np.concatenate([-w1 * sine, -w1 * cosine], axis=0).T
    second = np.concatenate([-w2 * cosine, w2 * sine], axis=0).T
    low = lambda a: np.ascontiguousarray(a).astype(ml_dtypes.bfloat16)
    return low(forward), low(first), low(second)


@functools.lru_cache(maxsize=None)
def line_tables(length):
    half = length // 2
    modes = np.arange(half)
    angles = (2.0 * np.pi / length) * ((modes[:, None] * np.arange(length)[None, :]) % length)
    wave = (2.0 * np.pi / length) * modes
    weight = np.where(modes == 0, 1.0, 2.0) / length
    first = -(weight * wave) @ np.sin(angles)
    second = -(weight * wave * wave) @ np.cos(angles)
    gap = np.arange(half)[None, :] - np.arange(half)[:, None]
    made = []
    for row in (first, second):
        a, b = row[gap % length], row[(gap + half) % length]
        made += [0.5 * (a + b), 0.5 * (a - b)]
    every = np.stack(made).reshape(4, half, half // TILE, TILE).transpose(2, 0, 1, 3)
    return np.ascontiguousarray(every).astype(ml_dtypes.bfloat16)


CHUNKS = 4
SUB = 64
GATE_FLOPS = 10**10


def params(mib=VMEM_MIB, **more):
    return pltpu.CompilerParams(vmem_limit_bytes=mib * 1024 * 1024, **more)


def begin(copies, sems, first=0):
    made = [pltpu.make_async_copy(src, dst, sems.at[first + n]) for n, (src, dst) in enumerate(copies)]
    for copy in made:
        copy.start()
    return made


def finish_all(made):
    for copy in made:
        copy.wait()


def full(shape):
    return pl.BlockSpec(shape, lambda i: (0,) * len(shape))


SMEM = pl.BlockSpec(memory_space=pltpu.SMEM)
HBM = pl.BlockSpec(memory_space=pltpu.HBM)
SMALL = pl.BlockSpec(memory_space=pltpu.VMEM)
near_by = functools.partial(pltpu.with_memory_space_constraint, memory_space=pltpu.VMEM)
far_off = functools.partial(pltpu.with_memory_space_constraint, memory_space=pltpu.HBM)


def dot(a, b):
    return jnp.dot(a, b, preferred_element_type=f32)


def pack_kernel(adj, wind, send, l0, l1, l2, adj_v, wind_v, send_v, lows_v, sem_in, sem_out):
    parts, _, rows, _ = send.shape
    per = parts // CHUNKS
    loads, stores = [], []
    for k in range(CHUNKS):
        at = pl.ds(k * per * rows, per * rows)
        loads.append(begin([(adj.at[:, at], adj_v.at[:, at]), (wind.at[1, at], wind_v.at[at])], sem_in, 2 * k))
    for k in range(CHUNKS):
        finish_all(loads[k])
        for s in range(k * per, (k + 1) * per):
            at = slice(s * rows, (s + 1) * rows)
            for c in range(3):
                low = adj_v[c, at].astype(bf16)
                send_v[s, c] = low
                lows_v[c, at] = low
            send_v[s, 3] = wind_v[at]
        at, part = pl.ds(k * per * rows, per * rows), pl.ds(k * per, per)
        stores += begin([(send_v.at[part], send.at[part])]
                        + [(lows_v.at[c, at], low.at[at]) for c, low in enumerate((l0, l1, l2))], sem_out, 4 * k)
    finish_all(stores)


def pack(adj, wind, parts):
    _, nx, ny = adj.shape
    rows = nx // parts
    sent, kept = (parts, 4, rows, ny), (3, nx, ny)
    return pl.pallas_call(
        pack_kernel,
        in_specs=[HBM, HBM],
        out_specs=[HBM] * 4,
        out_shape=[pltpu.HBM(sent, bf16)] + [pltpu.HBM((nx, ny), bf16)] * 3,
        scratch_shapes=[pltpu.VMEM(kept, f32), pltpu.VMEM((nx, ny), bf16), pltpu.VMEM(sent, bf16), pltpu.VMEM(kept, bf16),
                        pltpu.SemaphoreType.DMA((2 * CHUNKS,)), pltpu.SemaphoreType.DMA((4 * CHUNKS,))],
        compiler_params=params(),
        cost_estimate=pl.CostEstimate(flops=0, bytes_accessed=nx * ny * 32, transcendentals=0),
        name="pack",
    )(far_off(adj), far_off(wind))


def speed_of(w):
    return jnp.sqrt(w[0] * w[0] + w[1] * w[1] + w[2] * w[2])


def class_sums(column, cls, acc, count):
    for k in range(count):
        kept = jnp.where(cls == k, column, 0.0)
        acc[k] += jnp.sum(kept.reshape(-1, 8, kept.shape[-1]), axis=0)


def to_lanes(acc, count, offset):
    per = jnp.sum(acc[...], axis=1)
    per = jnp.sum(per, axis=1, keepdims=True)
    row = lax.broadcasted_iota(jnp.int32, (count, LANES), 0)
    lane = lax.broadcasted_iota(jnp.int32, (count, LANES), 1)
    return jnp.sum(jnp.where(lane == row + offset, per, 0.0), axis=0, keepdims=True)


def x_kernel(after, fwd, inv, l0, l1, l2, wind, rhs, low, spec, fwd_v, inv_v, wind_v, rhs_v, sem_l, sem_f, sem_i, sem_o):
    nx, ny = l0.shape
    steps = nx // TILE
    ats = [pl.ds(t * TILE, TILE) for t in range(steps)]
    lines = begin([(ref, low.at[:, pl.ds(c * ny, ny)]) for c, ref in enumerate((l0, l1, l2))], sem_l)
    tiles = begin([(fwd.at[at], fwd_v.at[at]) for at in ats], sem_f)
    loads = [begin([(inv.at[t], inv_v.at[t]), (wind.at[0, at], wind_v.at[at])], sem_i, 2 * t) for t, at in enumerate(ats)]
    finish_all(lines)
    for t in range(0, steps, 2):
        finish_all(tiles[t:t + 2])
        at = slice(t * TILE, (t + 2) * TILE)
        spec[at] = dot(fwd_v[at], low[...]).astype(bf16)
    stores = []
    for t, at in enumerate(ats):
        finish_all(loads[t])
        both = dot(inv_v[t], spec[...])
        for r in range(0, TILE, SUB):
            sub = slice(t * TILE + r, t * TILE + r + SUB)
            w0 = wind_v[sub].astype(f32)
            for c in range(3):
                cols = slice(c * ny, (c + 1) * ny)
                rhs_v[c, sub] = w0 * both[r:r + SUB, cols] + viscosity * both[TILE + r:TILE + r + SUB, cols]
        stores += begin([(rhs_v.at[:, at], rhs.at[:, at])], sem_o, t)
    finish_all(stores)


def x_part(after, fwd, inv, lows, wind):
    _, nx, ny = wind.shape
    steps = nx // TILE
    dma = pltpu.SemaphoreType.DMA
    return pl.pallas_call(
        x_kernel,
        in_specs=[SMEM] + [HBM] * 6,
        out_specs=HBM,
        out_shape=pltpu.HBM((3, nx, ny), f32),
        scratch_shapes=[pltpu.VMEM((nx, 3 * ny), bf16), pltpu.VMEM((nx, 3 * ny), bf16),
                        pltpu.VMEM(fwd.shape, bf16), pltpu.VMEM(inv.shape, bf16),
                        pltpu.VMEM((nx, ny), bf16), pltpu.VMEM((3, nx, ny), f32),
                        dma((3,)), dma((steps,)), dma((2 * steps,)), dma((steps,))],
        compiler_params=params(32),
        cost_estimate=pl.CostEstimate(flops=6 * nx * nx * 3 * ny, bytes_accessed=12 * 1024 * 1024, transcendentals=0),
        name="x_part",
    )(after, far_off(fwd), far_off(inv), *[far_off(low) for low in lows], far_off(wind))


def y_kernel(after, recv, table_v, out, plus, minus, out_v, sem_o):
    parts, _, rows, ny = recv.shape
    half, steps = parts // 2, table_v.shape[0]
    for s in range(half):
        for c in range(3):
            u, v = recv[s, c].astype(f32), recv[s + half, c].astype(f32)
            at = (slice(c * rows, (c + 1) * rows), slice(s * ny, (s + 1) * ny))
            plus[at] = (u + v).astype(bf16)
            minus[at] = (u - v).astype(bf16)
    per = TILE // ny
    stores = []
    for t in range(steps):
        p1, q1 = dot(plus[...], table_v[t, 0]), dot(minus[...], table_v[t, 1])
        p2, q2 = dot(plus[...], table_v[t, 2]), dot(minus[...], table_v[t, 3])
        for s in range(per):
            cols = slice(s * ny, (s + 1) * ny)
            a, b = t * per + s, half + t * per + s
            for r in range(0, rows, SUB):
                sub = slice(r, r + SUB)
                wa, wb = recv[a, 3, sub].astype(f32), recv[b, 3, sub].astype(f32)
                for c in range(3):
                    at = slice(c * rows + r, c * rows + r + SUB)
                    u1, v1, u2, v2 = (m[at, cols] for m in (p1, q1, p2, q2))
                    out_v[a, c, sub] = (wa * (u1 + v1) + viscosity * (u2 + v2)).astype(bf16)
                    out_v[b, c, sub] = (wb * (u1 - v1) + viscosity * (u2 - v2)).astype(bf16)
        ends = [pl.ds(base, per) for base in (t * per, half + t * per)]
        stores += begin([(out_v.at[e], out.at[e]) for e in ends], sem_o, 2 * t)
    finish_all(stores)


def y_part(after, recv, table):
    parts, _, rows, ny = recv.shape
    n, steps = parts * ny, table.shape[0]
    sent = (parts, 3, rows, ny)
    dma = pltpu.SemaphoreType.DMA
    return pl.pallas_call(
        y_kernel,
        in_specs=[HBM, SMALL, SMALL],
        out_specs=HBM,
        out_shape=pltpu.HBM(sent, bf16),
        scratch_shapes=[pltpu.VMEM((3 * rows, n // 2), bf16), pltpu.VMEM((3 * rows, n // 2), bf16),
                        pltpu.VMEM(sent, bf16), dma((2 * steps,))],
        compiler_params=params(),
        cost_estimate=pl.CostEstimate(flops=2 * n * n * 3 * rows, bytes_accessed=4 * 1024 * 1024, transcendentals=0),
        name="y_part",
    )(far_off(after), near_by(recv), near_by(table))


def gate_kernel(early, q0, q1, q2, out):
    out[...] = early[...]


def gate(early, far):
    return pl.pallas_call(
        gate_kernel,
        in_specs=[SMALL, HBM, HBM, SMALL],
        out_specs=SMALL,
        out_shape=jax.ShapeDtypeStruct(early.shape, f32),
        compiler_params=params(4),
        cost_estimate=pl.CostEstimate(flops=GATE_FLOPS, bytes_accessed=1024, transcendentals=0),
        name="gate",
    )(early, *[far_off(q) for q in far[:2]], near_by(far[2]))


def local_kernel(count, scal, coef, part, wind, classes, adj, p0, p1, p2, q0, rhs, sums,
                 part_v, wind_v, cls_v, adj_v, near_v, far_v, first, second, top, sem_in, sem_out):
    nx, ny = classes.shape
    rows = nx // CHUNKS
    loads, stores = [], []
    for k in range(CHUNKS):
        at = pl.ds(k * rows, rows)
        loads.append(begin([(a.at[:, at], b.at[:, at]) for a, b in ((wind, wind_v), (part, part_v), (adj, adj_v))]
                           + [(classes.at[at], cls_v.at[at]), (q0.at[at], far_v.at[at])]
                           + [(p.at[at], near_v.at[c, at]) for c, p in enumerate((p0, p1, p2))], sem_in, 8 * k))
    for ref in (first, second, top):
        ref[...] = jnp.zeros_like(ref)
    for k in range(CHUNKS):
        finish_all(loads[k])
        for n in range(k * rows // SUB, (k + 1) * rows // SUB):
            at = slice(n * SUB, (n + 1) * SUB)
            cls = cls_v[at]
            w = [wind_v[c, at].astype(f32) for c in range(3)]
            size = jnp.abs(w[0]) + jnp.abs(w[1]) + jnp.abs(w[2])
            top[...] = jnp.maximum(top[...], jnp.max(size.reshape(-1, 8, ny), axis=0))
            weight = scal[0] * speed_of(w)
            drag = jnp.zeros_like(weight)
            for m in range(count):
                drag = jnp.where(cls == m, coef[m], drag)
            damp = drag * weight + 2.0 * viscosity
            slope = (0.5 * scal[1]) * w[2]
            held, moved = jnp.zeros_like(weight), jnp.zeros_like(weight)
            for c in range(3):
                a = adj_v[c, at]
                r = part_v[c, at] - damp * a + (viscosity + slope) * near_v[c, at].astype(f32)
                if c == 0:
                    r += (viscosity - slope) * far_v[at].astype(f32)
                part_v[c, at] = r
                held += a * w[c]
                moved += r * w[c]
            class_sums(weight * held, cls, first, count)
            class_sums(weight * moved, cls, second, count)
        at = pl.ds(k * rows, rows)
        stores += begin([(part_v.at[:, at], rhs.at[:, at])], sem_out, k)
    lane = lax.broadcasted_iota(jnp.int32, (1, LANES), 1)
    peak = jnp.max(jnp.max(top[...], axis=0, keepdims=True), axis=1, keepdims=True)
    both = to_lanes(first, count, 0) + to_lanes(second, count, count)
    sums[...] = jnp.where(lane == 2 * count, peak, both)
    finish_all(stores)


def local_part(scal, coef, part, wind, classes, adj, near, far):
    _, nx, ny = part.shape
    count = coef.shape[0]
    whole = (3, nx, ny)
    dma = pltpu.SemaphoreType.DMA
    return pl.pallas_call(
        functools.partial(local_kernel, count),
        in_specs=[SMEM, SMEM] + [HBM] * 8,
        out_specs=[HBM, SMALL],
        out_shape=[pltpu.HBM(whole, f32), jax.ShapeDtypeStruct((1, LANES), f32)],
        scratch_shapes=[pltpu.VMEM(whole, f32), pltpu.VMEM(whole, bf16), pltpu.VMEM((nx, ny), jnp.int32),
                        pltpu.VMEM(whole, f32), pltpu.VMEM(whole, bf16), pltpu.VMEM((nx, ny), bf16),
                        pltpu.VMEM((count, 8, ny), f32), pltpu.VMEM((count, 8, ny), f32), pltpu.VMEM((8, ny), f32),
                        dma((8 * CHUNKS,)), dma((CHUNKS,))],
        compiler_params=params(),
        cost_estimate=pl.CostEstimate(flops=200 * nx * ny, bytes_accessed=8 * 1024 * 1024, transcendentals=0),
        name="local_part",
    )(scal, coef, *[far_off(a) for a in (part, wind, classes, adj, *near, far)])


def join_kernel(count, scal, early, part, wind, classes, q1, q2, drift, rhs, sums,
                wind_v, cls_v, far_v, acc, sem_in):
    parts, _, rows, _ = drift.shape
    per = parts // CHUNKS
    loads = []
    for k in range(CHUNKS):
        at = pl.ds(k * per * rows, per * rows)
        loads.append(begin([(wind.at[:, at], wind_v.at[:, at]), (classes.at[at], cls_v.at[at]),
                            (part.at[:, at], rhs.at[:, at]), (q1.at[at], far_v.at[at])], sem_in, 4 * k))
    acc[...] = jnp.zeros_like(acc)
    for k in range(CHUNKS):
        finish_all(loads[k])
        for n in range(k * per * rows // SUB, (k + 1) * per * rows // SUB):
            at = slice(n * SUB, (n + 1) * SUB)
            s, sub = n * SUB // rows, slice(n * SUB % rows, n * SUB % rows + SUB)
            w = [wind_v[c, at].astype(f32) for c in range(3)]
            down = viscosity - (0.5 * scal[1]) * w[2]
            total = jnp.zeros_like(down)
            for c in range(3):
                r = drift[s, c, sub].astype(f32)
                if c > 0:
                    r += down * (far_v[at] if c == 1 else q2[at]).astype(f32)
                rhs[c, at] = rhs[c, at] + r
                total += r * w[c]
            class_sums(scal[0] * speed_of(w) * total, cls_v[at], acc, count)
    sums[...] = jnp.broadcast_to((early[...] + to_lanes(acc, count, count))[None], sums.shape)


def join(scal, early, part, wind, classes, far, drift, count):
    parts, _, rows, ny = drift.shape
    nx = parts * rows
    whole = (3, nx, ny)
    dma = pltpu.SemaphoreType.DMA
    return pl.pallas_call(
        functools.partial(join_kernel, count),
        in_specs=[SMEM, SMALL] + [HBM] * 4 + [SMALL] * 2,
        out_specs=[SMALL, SMALL],
        out_shape=[pltpu.VMEM(whole, f32), jax.ShapeDtypeStruct((2 * parts, 1, LANES), f32)],
        scratch_shapes=[pltpu.VMEM(whole, bf16), pltpu.VMEM((nx, ny), jnp.int32), pltpu.VMEM((nx, ny), bf16),
                        pltpu.VMEM((count, 8, ny), f32), dma((4 * CHUNKS,))],
        compiler_params=params(),
        cost_estimate=pl.CostEstimate(flops=100 * nx * ny, bytes_accessed=8 * 1024 * 1024, transcendentals=0),
        name="join",
    )(scal, early, *[far_off(a) for a in (part, wind, classes, far[0])], near_by(far[1]), near_by(drift))


def merge(rows, count):
    lane = lax.broadcasted_iota(jnp.int32, (1, LANES), 1)
    return jnp.where(lane == 2 * count, jnp.max(rows, axis=0), jnp.sum(rows, axis=0))


def fold_kernel(count, got, out):
    out[...] = jnp.broadcast_to(merge(got[...], count)[None], out.shape)


def fold(got, size, count):
    return pl.pallas_call(
        functools.partial(fold_kernel, count),
        out_shape=jax.ShapeDtypeStruct((size, 1, LANES), f32),
        compiler_params=params(4),
        name="fold",
    )(got)


def finish_kernel(count, scale, got, adj, rhs, new, sens, new_v, sems):
    nx = adj.shape[1]
    rows = nx // CHUNKS
    sums = merge(got[...], count)
    lane = lax.broadcasted_iota(jnp.int32, (1, LANES), 1)
    top = jnp.max(jnp.where(lane == 2 * count, sums, 0.0), axis=1, keepdims=True)
    step = courant / (top + epsilon)
    stores = []
    for k in range(CHUNKS):
        at = slice(k * rows, (k + 1) * rows)
        for c in range(3):
            new_v[c, at] = adj[c, at] + step * rhs[c, at]
        at = pl.ds(k * rows, rows)
        stores += begin([(new_v.at[:, at], new.at[:, at])], sems, k)
    later = pltpu.roll(sums, LANES - count, 1)
    sens[...] = (-step * scale * (sums + step * later))[:, :count]
    finish_all(stores)


def finish(got, adj, rhs, count, scale):
    return pl.pallas_call(
        functools.partial(finish_kernel, count, scale),
        in_specs=[SMALL, SMALL, SMALL],
        out_specs=[HBM, SMALL],
        out_shape=[pltpu.HBM(adj.shape, f32), jax.ShapeDtypeStruct((1, count), f32)],
        scratch_shapes=[pltpu.VMEM(adj.shape, f32), pltpu.SemaphoreType.DMA((CHUNKS,))],
        compiler_params=params(),
        cost_estimate=pl.CostEstimate(flops=2 * adj.size, bytes_accessed=12 * adj.size, transcendentals=0),
        name="finish",
    )(got, near_by(adj), near_by(rhs))


def swap(x, axes, groups=None):
    return lax.all_to_all(x, axes, split_axis=0, concat_axis=0, axis_index_groups=groups, tiled=True)


def local(adjoint, wind, classes, drag_coef):
    gz, gy = lax.axis_size("gz"), lax.axis_size("gy")
    _, _, nx, ny = adjoint.shape
    total_y = ny * gy
    count = drag_coef.shape[0]
    adj = adjoint.reshape(3, nx, ny)
    wnd = wind.reshape(3, nx, ny)

    fx, d1x, d2x = tables(nx)
    inv_x = np.concatenate([d1x.reshape(-1, TILE, nx), d2x.reshape(-1, TILE, nx)], axis=1)

    me = lax.axis_index("gz")
    height = jnp.exp(-2.0 * (me.astype(f32) + 0.5) / gz)
    sign = jnp.where(me % 2 == 0, 1.0, -1.0).astype(f32)
    scal = jnp.stack([height, sign])

    send, *lows = pack(adj, wnd, gy)
    recv = swap(send, "gy")

    pair = [(i, i ^ 1) for i in range(gz)]
    onward = [(i, i + 2) for i in range(0, gz - 2, 2)] + [(i, i - 2) for i in range(3, gz, 2)]
    near = [lax.ppermute(low, "gz", pair) for low in lows]
    far = [lax.ppermute(low, "gz", onward) for low in near]

    part = x_part(scal, jnp.asarray(fx), jnp.asarray(inv_x), lows, wnd)
    drift = swap(y_part(part, recv, jnp.asarray(line_tables(total_y))), "gy")
    part, early = local_part(scal, drag_coef, part, wnd, classes, adj, near, far[0])
    rhs, sums = join(scal, gate(early, far), part, wnd, classes, far[1:], drift, count)

    group, pairs = 2 * gy, gz // 2
    within = [[k * group + i for i in range(group)] for k in range(pairs)]
    across = [[k * group + i for k in range(pairs)] for i in range(group)]
    got = swap(fold(swap(sums, ("gz", "gy"), within), pairs, count), ("gz", "gy"), across)
    scale = 1.0 / math.sqrt(nx * total_y * gz / count)
    new, sens = finish(got, adj, rhs, count, scale)
    return new.reshape(adjoint.shape), sens.reshape(count)


def solution(mesh):
    return jax.shard_map(
        local,
        mesh=mesh,
        in_specs=(P(None, "gz", None, "gy"), P(None, "gz", None, "gy"), P(None, "gy"), P()),
        out_specs=(P(None, "gz", None, "gy"), P()),
        check_vma=False,
    )
```

```python
import functools
import math

import jax
import jax.numpy as jnp
import ml_dtypes
import numpy as np
from jax import lax
from jax.experimental import pallas as pl
from jax.experimental.pallas import tpu as pltpu
from jax.sharding import PartitionSpec as P

viscosity = 0.3
courant = 0.8
epsilon = 1e-06
LANES = 128
TILE = 256
VMEM_MIB = 16
f32 = jnp.float32
bf16 = jnp.bfloat16


@functools.lru_cache(maxsize=None)
def tables(length):
    half = length // 2
    modes = np.arange(half)
    points = np.arange(length)
    angles = (2.0 * np.pi / length) * ((modes[:, None] * points[None, :]) % length)
    cosine, sine = np.cos(angles), np.sin(angles)
    forward = np.concatenate([cosine, -sine], axis=0)
    wave = (2.0 * np.pi / length) * modes
    weight = np.where(modes == 0, 1.0, 2.0) / length
    w1, w2 = (weight * wave)[:, None], (weight * wave * wave)[:, None]
    first = np.concatenate([-w1 * sine, -w1 * cosine], axis=0).T
    second = np.concatenate([-w2 * cosine, w2 * sine], axis=0).T
    low = lambda a: np.ascontiguousarray(a).astype(ml_dtypes.bfloat16)
    return low(forward), low(first), low(second)


@functools.lru_cache(maxsize=None)
def line_tables(length):
    half = length // 2
    modes = np.arange(half)
    angles = (2.0 * np.pi / length) * ((modes[:, None] * np.arange(length)[None, :]) % length)
    wave = (2.0 * np.pi / length) * modes
    weight = np.where(modes == 0, 1.0, 2.0) / length
    first = -(weight * wave) @ np.sin(angles)
    second = -(weight * wave * wave) @ np.cos(angles)
    gap = np.arange(half)[None, :] - np.arange(half)[:, None]
    made = []
    for row in (first, second):
        a, b = row[gap % length], row[(gap + half) % length]
        made += [0.5 * (a + b), 0.5 * (a - b)]
    every = np.stack(made).reshape(4, half, half // TILE, TILE).transpose(2, 0, 1, 3)
    return np.ascontiguousarray(every).astype(ml_dtypes.bfloat16)


CHUNKS = 4
SUB = 64
GATE_FLOPS = 10**10


def params(mib=VMEM_MIB, **more):
    return pltpu.CompilerParams(vmem_limit_bytes=mib * 1024 * 1024, **more)


def begin(copies, sems, first=0):
    made = [pltpu.make_async_copy(src, dst, sems.at[first + n]) for n, (src, dst) in enumerate(copies)]
    for copy in made:
        copy.start()
    return made


def finish_all(made):
    for copy in made:
        copy.wait()


def full(shape):
    return pl.BlockSpec(shape, lambda i: (0,) * len(shape))


SMEM = pl.BlockSpec(memory_space=pltpu.SMEM)
HBM = pl.BlockSpec(memory_space=pltpu.HBM)
SMALL = pl.BlockSpec(memory_space=pltpu.VMEM)
near_by = functools.partial(pltpu.with_memory_space_constraint, memory_space=pltpu.VMEM)
far_off = functools.partial(pltpu.with_memory_space_constraint, memory_space=pltpu.HBM)


def dot(a, b):
    return jnp.dot(a, b, preferred_element_type=f32)


def pack_kernel(adj, wind, send, l0, l1, l2, adj_v, wind_v, send_v, lows_v, sem_in, sem_out):
    parts, _, rows, _ = send.shape
    per = parts // CHUNKS
    loads, stores = [], []
    for k in range(CHUNKS):
        at = pl.ds(k * per * rows, per * rows)
        loads.append(begin([(adj.at[:, at], adj_v.at[:, at]), (wind.at[1, at], wind_v.at[at])], sem_in, 2 * k))
    for k in range(CHUNKS):
        finish_all(loads[k])
        for s in range(k * per, (k + 1) * per):
            at = slice(s * rows, (s + 1) * rows)
            for c in range(3):
                low = adj_v[c, at].astype(bf16)
                send_v[s, c] = low
                lows_v[c, at] = low
            send_v[s, 3] = wind_v[at]
        at, part = pl.ds(k * per * rows, per * rows), pl.ds(k * per, per)
        stores += begin([(send_v.at[part], send.at[part])]
                        + [(lows_v.at[c, at], low.at[at]) for c, low in enumerate((l0, l1, l2))], sem_out, 4 * k)
    finish_all(stores)


def pack(adj, wind, parts):
    _, nx, ny = adj.shape
    rows = nx // parts
    sent, kept = (parts, 4, rows, ny), (3, nx, ny)
    return pl.pallas_call(
        pack_kernel,
        in_specs=[HBM, HBM],
        out_specs=[HBM] * 4,
        out_shape=[pltpu.HBM(sent, bf16)] + [pltpu.HBM((nx, ny), bf16)] * 3,
        scratch_shapes=[pltpu.VMEM(kept, f32), pltpu.VMEM((nx, ny), bf16), pltpu.VMEM(sent, bf16), pltpu.VMEM(kept, bf16),
                        pltpu.SemaphoreType.DMA((2 * CHUNKS,)), pltpu.SemaphoreType.DMA((4 * CHUNKS,))],
        compiler_params=params(),
        cost_estimate=pl.CostEstimate(flops=0, bytes_accessed=nx * ny * 32, transcendentals=0),
        name="pack",
    )(far_off(adj), far_off(wind))


def speed_of(w):
    return jnp.sqrt(w[0] * w[0] + w[1] * w[1] + w[2] * w[2])


def class_sums(column, cls, acc, count):
    for k in range(count):
        kept = jnp.where(cls == k, column, 0.0)
        acc[k] += jnp.sum(kept.reshape(-1, 8, kept.shape[-1]), axis=0)


def to_lanes(acc, count, offset):
    per = jnp.sum(acc[...], axis=1)
    per = jnp.sum(per, axis=1, keepdims=True)
    row = lax.broadcasted_iota(jnp.int32, (count, LANES), 0)
    lane = lax.broadcasted_iota(jnp.int32, (count, LANES), 1)
    return jnp.sum(jnp.where(lane == row + offset, per, 0.0), axis=0, keepdims=True)


def x_kernel(after, fwd, inv, l0, l1, l2, wind, rhs, low, spec, fwd_v, inv_v, wind_v, rhs_v, sem_l, sem_f, sem_i, sem_o):
    nx, ny = l0.shape
    steps = nx // TILE
    ats = [pl.ds(t * TILE, TILE) for t in range(steps)]
    lines = begin([(ref, low.at[:, pl.ds(c * ny, ny)]) for c, ref in enumerate((l0, l1, l2))], sem_l)
    tiles = begin([(fwd.at[at], fwd_v.at[at]) for at in ats], sem_f)
    loads = [begin([(inv.at[t], inv_v.at[t]), (wind.at[0, at], wind_v.at[at])], sem_i, 2 * t) for t, at in enumerate(ats)]
    finish_all(lines)
    for t in range(0, steps, 2):
        finish_all(tiles[t:t + 2])
        at = slice(t * TILE, (t + 2) * TILE)
        spec[at] = dot(fwd_v[at], low[...]).astype(bf16)
    stores = []
    for t, at in enumerate(ats):
        finish_all(loads[t])
        both = dot(inv_v[t], spec[...])
        for r in range(0, TILE, SUB):
            sub = slice(t * TILE + r, t * TILE + r + SUB)
            w0 = wind_v[sub].astype(f32)
            for c in range(3):
                cols = slice(c * ny, (c + 1) * ny)
                rhs_v[c, sub] = w0 * both[r:r + SUB, cols] + viscosity * both[TILE + r:TILE + r + SUB, cols]
        stores += begin([(rhs_v.at[:, at], rhs.at[:, at])], sem_o, t)
    finish_all(stores)


def x_part(after, fwd, inv, lows, wind):
    _, nx, ny = wind.shape
    steps = nx // TILE
    dma = pltpu.SemaphoreType.DMA
    return pl.pallas_call(
        x_kernel,
        in_specs=[SMEM] + [HBM] * 6,
        out_specs=HBM,
        out_shape=pltpu.HBM((3, nx, ny), f32),
        scratch_shapes=[pltpu.VMEM((nx, 3 * ny), bf16), pltpu.VMEM((nx, 3 * ny), bf16),
                        pltpu.VMEM(fwd.shape, bf16), pltpu.VMEM(inv.shape, bf16),
                        pltpu.VMEM((nx, ny), bf16), pltpu.VMEM((3, nx, ny), f32),
                        dma((3,)), dma((steps,)), dma((2 * steps,)), dma((steps,))],
        compiler_params=params(32),
        cost_estimate=pl.CostEstimate(flops=6 * nx * nx * 3 * ny, bytes_accessed=12 * 1024 * 1024, transcendentals=0),
        name="x_part",
    )(after, far_off(fwd), far_off(inv), *[far_off(low) for low in lows], far_off(wind))


def y_kernel(after, recv, table_v, out, plus, minus, out_v, sem_o):
    parts, _, rows, ny = recv.shape
    half, steps = parts // 2, table_v.shape[0]
    for s in range(half):
        for c in range(3):
            u, v = recv[s, c].astype(f32), recv[s + half, c].astype(f32)
            at = (slice(c * rows, (c + 1) * rows), slice(s * ny, (s + 1) * ny))
            plus[at] = (u + v).astype(bf16)
            minus[at] = (u - v).astype(bf16)
    per = TILE // ny
    stores = []
    for t in range(steps):
        p1, q1 = dot(plus[...], table_v[t, 0]), dot(minus[...], table_v[t, 1])
        p2, q2 = dot(plus[...], table_v[t, 2]), dot(minus[...], table_v[t, 3])
        for s in range(per):
            cols = slice(s * ny, (s + 1) * ny)
            a, b = t * per + s, half + t * per + s
            for r in range(0, rows, SUB):
                sub = slice(r, r + SUB)
                wa, wb = recv[a, 3, sub].astype(f32), recv[b, 3, sub].astype(f32)
                for c in range(3):
                    at = slice(c * rows + r, c * rows + r + SUB)
                    u1, v1, u2, v2 = (m[at, cols] for m in (p1, q1, p2, q2))
                    out_v[a, c, sub] = (wa * (u1 + v1) + viscosity * (u2 + v2)).astype(bf16)
                    out_v[b, c, sub] = (wb * (u1 - v1) + viscosity * (u2 - v2)).astype(bf16)
        ends = [pl.ds(base, per) for base in (t * per, half + t * per)]
        stores += begin([(out_v.at[e], out.at[e]) for e in ends], sem_o, 2 * t)
    finish_all(stores)


def y_part(after, recv, table):
    parts, _, rows, ny = recv.shape
    n, steps = parts * ny, table.shape[0]
    sent = (parts, 3, rows, ny)
    dma = pltpu.SemaphoreType.DMA
    return pl.pallas_call(
        y_kernel,
        in_specs=[HBM, SMALL, SMALL],
        out_specs=HBM,
        out_shape=pltpu.HBM(sent, bf16),
        scratch_shapes=[pltpu.VMEM((3 * rows, n // 2), bf16), pltpu.VMEM((3 * rows, n // 2), bf16),
                        pltpu.VMEM(sent, bf16), dma((2 * steps,))],
        compiler_params=params(),
        cost_estimate=pl.CostEstimate(flops=2 * n * n * 3 * rows, bytes_accessed=4 * 1024 * 1024, transcendentals=0),
        name="y_part",
    )(far_off(after), near_by(recv), near_by(table))


def gate_kernel(early, q0, q1, q2, out):
    out[...] = early[...]


def gate(early, far):
    return pl.pallas_call(
        gate_kernel,
        in_specs=[SMALL, HBM, HBM, SMALL],
        out_specs=SMALL,
        out_shape=jax.ShapeDtypeStruct(early.shape, f32),
        compiler_params=params(4),
        cost_estimate=pl.CostEstimate(flops=GATE_FLOPS, bytes_accessed=1024, transcendentals=0),
        name="gate",
    )(early, *[far_off(q) for q in far[:2]], near_by(far[2]))


def local_kernel(count, scal, coef, part, wind, classes, adj, p0, p1, p2, q0, rhs, sums,
                 part_v, wind_v, cls_v, adj_v, near_v, far_v, first, second, top, sem_in, sem_out):
    nx, ny = classes.shape
    rows = nx // CHUNKS
    loads, stores = [], []
    for k in range(CHUNKS):
        at = pl.ds(k * rows, rows)
        loads.append(begin([(a.at[:, at], b.at[:, at]) for a, b in ((wind, wind_v), (part, part_v), (adj, adj_v))]
                           + [(classes.at[at], cls_v.at[at]), (q0.at[at], far_v.at[at])]
                           + [(p.at[at], near_v.at[c, at]) for c, p in enumerate((p0, p1, p2))], sem_in, 8 * k))
    for ref in (first, second, top):
        ref[...] = jnp.zeros_like(ref)
    for k in range(CHUNKS):
        finish_all(loads[k])
        for n in range(k * rows // SUB, (k + 1) * rows // SUB):
            at = slice(n * SUB, (n + 1) * SUB)
            cls = cls_v[at]
            w = [wind_v[c, at].astype(f32) for c in range(3)]
            size = jnp.abs(w[0]) + jnp.abs(w[1]) + jnp.abs(w[2])
            top[...] = jnp.maximum(top[...], jnp.max(size.reshape(-1, 8, ny), axis=0))
            weight = scal[0] * speed_of(w)
            drag = jnp.zeros_like(weight)
            for m in range(count):
                drag = jnp.where(cls == m, coef[m], drag)
            damp = drag * weight + 2.0 * viscosity
            slope = (0.5 * scal[1]) * w[2]
            held, moved = jnp.zeros_like(weight), jnp.zeros_like(weight)
            for c in range(3):
                a = adj_v[c, at]
                r = part_v[c, at] - damp * a + (viscosity + slope) * near_v[c, at].astype(f32)
                if c == 0:
                    r += (viscosity - slope) * far_v[at].astype(f32)
                part_v[c, at] = r
                held += a * w[c]
                moved += r * w[c]
            class_sums(weight * held, cls, first, count)
            class_sums(weight * moved, cls, second, count)
        at = pl.ds(k * rows, rows)
        stores += begin([(part_v.at[:, at], rhs.at[:, at])], sem_out, k)
    lane = lax.broadcasted_iota(jnp.int32, (1, LANES), 1)
    peak = jnp.max(jnp.max(top[...], axis=0, keepdims=True), axis=1, keepdims=True)
    both = to_lanes(first, count, 0) + to_lanes(second, count, count)
    sums[...] = jnp.where(lane == 2 * count, peak, both)
    finish_all(stores)


def local_part(scal, coef, part, wind, classes, adj, near, far):
    _, nx, ny = part.shape
    count = coef.shape[0]
    whole = (3, nx, ny)
    dma = pltpu.SemaphoreType.DMA
    return pl.pallas_call(
        functools.partial(local_kernel, count),
        in_specs=[SMEM, SMEM] + [HBM] * 8,
        out_specs=[HBM, SMALL],
        out_shape=[pltpu.HBM(whole, f32), jax.ShapeDtypeStruct((1, LANES), f32)],
        scratch_shapes=[pltpu.VMEM(whole, f32), pltpu.VMEM(whole, bf16), pltpu.VMEM((nx, ny), jnp.int32),
                        pltpu.VMEM(whole, f32), pltpu.VMEM(whole, bf16), pltpu.VMEM((nx, ny), bf16),
                        pltpu.VMEM((count, 8, ny), f32), pltpu.VMEM((count, 8, ny), f32), pltpu.VMEM((8, ny), f32),
                        dma((8 * CHUNKS,)), dma((CHUNKS,))],
        compiler_params=params(),
        cost_estimate=pl.CostEstimate(flops=200 * nx * ny, bytes_accessed=8 * 1024 * 1024, transcendentals=0),
        name="local_part",
    )(scal, coef, *[far_off(a) for a in (part, wind, classes, adj, *near, far)])


def join_kernel(count, scal, early, part, wind, cls_v, q1, q2, drift, rhs, sums,
                wind_v, far_v, acc, sem_in):
    parts, _, rows, _ = drift.shape
    per = parts // CHUNKS
    loads = []
    for k in range(CHUNKS):
        at = pl.ds(k * per * rows, per * rows)
        loads.append(begin([(wind.at[:, at], wind_v.at[:, at]), (part.at[:, at], rhs.at[:, at]), (q1.at[at], far_v.at[at])], sem_in, 3 * k))
    acc[...] = jnp.zeros_like(acc)
    for k in range(CHUNKS):
        finish_all(loads[k])
        for n in range(k * per * rows // SUB, (k + 1) * per * rows // SUB):
            at = slice(n * SUB, (n + 1) * SUB)
            s, sub = n * SUB // rows, slice(n * SUB % rows, n * SUB % rows + SUB)
            w = [wind_v[c, at].astype(f32) for c in range(3)]
            down = viscosity - (0.5 * scal[1]) * w[2]
            total = jnp.zeros_like(down)
            for c in range(3):
                r = drift[s, c, sub].astype(f32)
                if c > 0:
                    r += down * (far_v[at] if c == 1 else q2[at]).astype(f32)
                rhs[c, at] = rhs[c, at] + r
                total += r * w[c]
            class_sums(scal[0] * speed_of(w) * total, cls_v[at], acc, count)
    sums[...] = jnp.broadcast_to((early[...] + to_lanes(acc, count, count))[None], sums.shape)


def join(scal, early, part, wind, classes, far, drift, count):
    parts, _, rows, ny = drift.shape
    nx = parts * rows
    whole = (3, nx, ny)
    dma = pltpu.SemaphoreType.DMA
    return pl.pallas_call(
        functools.partial(join_kernel, count),
        in_specs=[SMEM, SMALL, HBM, HBM, SMALL, HBM, SMALL, SMALL],
        out_specs=[SMALL, SMALL],
        out_shape=[pltpu.VMEM(whole, f32), jax.ShapeDtypeStruct((2 * parts, 1, LANES), f32)],
        scratch_shapes=[pltpu.VMEM(whole, bf16), pltpu.VMEM((nx, ny), bf16),
                        pltpu.VMEM((count, 8, ny), f32), dma((3 * CHUNKS,))],
        compiler_params=params(),
        cost_estimate=pl.CostEstimate(flops=100 * nx * ny, bytes_accessed=8 * 1024 * 1024, transcendentals=0),
        name="join",
    )(scal, early, far_off(part), far_off(wind), near_by(classes), far_off(far[0]), near_by(far[1]), near_by(drift))


def merge(rows, count):
    lane = lax.broadcasted_iota(jnp.int32, (1, LANES), 1)
    return jnp.where(lane == 2 * count, jnp.max(rows, axis=0), jnp.sum(rows, axis=0))


def fold_kernel(count, got, out):
    out[...] = jnp.broadcast_to(merge(got[...], count)[None], out.shape)


def fold(got, size, count):
    return pl.pallas_call(
        functools.partial(fold_kernel, count),
        out_shape=jax.ShapeDtypeStruct((size, 1, LANES), f32),
        compiler_params=params(4),
        name="fold",
    )(got)


def finish_kernel(count, scale, got, adj, rhs, new, sens, new_v, sems):
    nx = adj.shape[1]
    rows = nx // CHUNKS
    sums = merge(got[...], count)
    lane = lax.broadcasted_iota(jnp.int32, (1, LANES), 1)
    top = jnp.max(jnp.where(lane == 2 * count, sums, 0.0), axis=1, keepdims=True)
    step = courant / (top + epsilon)
    stores = []
    for k in range(CHUNKS):
        at = slice(k * rows, (k + 1) * rows)
        for c in range(3):
            new_v[c, at] = adj[c, at] + step * rhs[c, at]
        at = pl.ds(k * rows, rows)
        stores += begin([(new_v.at[:, at], new.at[:, at])], sems, k)
    later = pltpu.roll(sums, LANES - count, 1)
    sens[...] = (-step * scale * (sums + step * later))[:, :count]
    finish_all(stores)


def finish(got, adj, rhs, count, scale):
    return pl.pallas_call(
        functools.partial(finish_kernel, count, scale),
        in_specs=[SMALL, SMALL, SMALL],
        out_specs=[HBM, SMALL],
        out_shape=[pltpu.HBM(adj.shape, f32), jax.ShapeDtypeStruct((1, count), f32)],
        scratch_shapes=[pltpu.VMEM(adj.shape, f32), pltpu.SemaphoreType.DMA((CHUNKS,))],
        compiler_params=params(),
        cost_estimate=pl.CostEstimate(flops=2 * adj.size, bytes_accessed=12 * adj.size, transcendentals=0),
        name="finish",
    )(got, near_by(adj), near_by(rhs))


def swap(x, axes, groups=None):
    return lax.all_to_all(x, axes, split_axis=0, concat_axis=0, axis_index_groups=groups, tiled=True)


def local(adjoint, wind, classes, drag_coef):
    gz, gy = lax.axis_size("gz"), lax.axis_size("gy")
    _, _, nx, ny = adjoint.shape
    total_y = ny * gy
    count = drag_coef.shape[0]
    adj = adjoint.reshape(3, nx, ny)
    wnd = wind.reshape(3, nx, ny)

    fx, d1x, d2x = tables(nx)
    inv_x = np.concatenate([d1x.reshape(-1, TILE, nx), d2x.reshape(-1, TILE, nx)], axis=1)

    me = lax.axis_index("gz")
    height = jnp.exp(-2.0 * (me.astype(f32) + 0.5) / gz)
    sign = jnp.where(me % 2 == 0, 1.0, -1.0).astype(f32)
    scal = jnp.stack([height, sign])

    send, *lows = pack(adj, wnd, gy)
    recv = swap(send, "gy")

    pair = [(i, i ^ 1) for i in range(gz)]
    onward = [(i, i + 2) for i in range(0, gz - 2, 2)] + [(i, i - 2) for i in range(3, gz, 2)]
    near = [lax.ppermute(low, "gz", pair) for low in lows]
    far = [lax.ppermute(low, "gz", onward) for low in near]

    part = x_part(scal, jnp.asarray(fx), jnp.asarray(inv_x), lows, wnd)
    drift = swap(y_part(part, recv, jnp.asarray(line_tables(total_y))), "gy")
    part, early = local_part(scal, drag_coef, part, wnd, classes, adj, near, far[0])
    rhs, sums = join(scal, gate(early, far), part, wnd, classes, far[1:], drift, count)

    group, pairs = 2 * gy, gz // 2
    within = [[k * group + i for i in range(group)] for k in range(pairs)]
    across = [[k * group + i for k in range(pairs)] for i in range(group)]
    got = swap(fold(swap(sums, ("gz", "gy"), within), pairs, count), ("gz", "gy"), across)
    scale = 1.0 / math.sqrt(nx * total_y * gz / count)
    new, sens = finish(got, adj, rhs, count, scale)
    return new.reshape(adjoint.shape), sens.reshape(count)


def solution(mesh):
    return jax.shard_map(
        local,
        mesh=mesh,
        in_specs=(P(None, "gz", None, "gy"), P(None, "gz", None, "gy"), P(None, "gy"), P()),
        out_specs=(P(None, "gz", None, "gy"), P()),
        check_vma=False,
    )
```
